32 devices in a mesh: group: 2 (over y), col: 4 (over x, core), row: 4 (over z).
Axes of the slice: x: 2, y: 2, z: 4, core: 2. Of those that a mesh axis runs over, the one named last changes fastest.
Arguments:
- initial_rates: float32 [96, 4096], P('group', ('col', 'row')), parts along dimension 0, may hold values from -3 to 3
- stimulus: bfloat16 [3, 96, 4096], P(None, 'group', ('col', 'row')), parts along dimension 1, may hold values from -3 to 3
- tile_values: bfloat16 [1024, 128, 128], P(('col', 'row')), may hold values from -0.25 to 0.25
- tile_rows: int32 [16, 64], P(('col', 'row')), may hold values from 0 to 7, as said below
- tile_cols: int32 [16, 64], P(('col', 'row')), may hold values from 0 to 7
- tile_count: int32 [16], P(('col', 'row')), may hold values from 16 to 64, as said below
- cotangent: float32 [96, 4096], P('group', ('col', 'row')), parts along dimension 0, may hold values from -6 to 6
Outputs:
- final_rates: float32 [96, 4096], P('group', ('col', 'row')), parts along dimension 0
- rate_grad: float32 [96, 4096], P('group', ('col', 'row')), parts along dimension 0
- weight_grad: bfloat16 [2048, 128, 128], P(('group', 'col', 'row')), parts along dimension 0
The draws below stay inside these ranges and needn't reach their ends.
There are 2 independent parts, one for each index of `group`. The reference program is written for one: setup_inputs(seed, part) draws one part's arguments, and reference() takes and returns one part's arrays. A program takes and returns all parts, laid end to end along the dimension named above; an argument that names none is the same for every part. Nothing has to cross between parts.
Inputs may be any that keep to these rules, and one draw needn't show every extreme that they name: A list's (tile_rows, tile_cols) pairs are distinct. Slots 0 to tile_count[q] - 1 of list q are live, the others are ignored; some list has 64 live slots.
All inputs are finite; a program needn't handle non-finite values.
Results may differ from the reference program's by a relative error of at most 0.007.
Values may be sent and summed in bfloat16 or wider, within the bound.
No kernel may reach another device: no remote copies, remote signals or barrier semaphores. Data moves between devices by JAX's collectives and lax.ppermute only.
A program may use at most 128 MiB of HBM per device.

```python
import jax
import jax.numpy as jnp
from jax import lax

B = 48
OWN_T = 2
TILE = 128
STEPS = 3
CAP = 64
DEVS = 16
RB = 8
CB = 8
NEURONS = 4096
N_COL = 4
N_ROW = 4


def tile_places(key):
    device_keys = jax.random.split(key, N_COL * N_ROW)

    def per_device(sub_key):
        return jax.random.permutation(sub_key, RB * CB)[:CAP]
    return jax.vmap(per_device)(device_keys).astype(jnp.int32)


def draw_tile_rows(key, part):
    places = tile_places(key)
    return (places // CB).astype(jnp.int32)


def draw_tile_cols(key, part):
    places = tile_places(key)
    return (places % CB).astype(jnp.int32)


def draw_tile_count(key, part):
    key = jax.random.fold_in(key, 29)
    devices = N_COL * N_ROW
    count_key, place_key = jax.random.split(key)
    divisor = jax.random.randint(count_key, (devices,), 1, 5)
    counts = CAP // divisor
    busiest = jax.random.randint(place_key, (), 0, devices)
    return jnp.where(jnp.arange(devices) == busiest, CAP, counts).astype(jnp.int32)


def steps_of(key, extent, pieces, least, top_value):
    def one(position, blocks):
        heights = jax.random.uniform(jax.random.fold_in(jax.random.fold_in(key, 6), position), (blocks,), jnp.float32, least / len(pieces), top_value / len(pieces))
        return jnp.repeat(jnp.exp(heights), extent[position] // blocks).reshape((-1,) + (1,) * (len(extent) - position - 1))

    gain = one(*pieces[0])
    for cut in pieces[1:]:
        gain = gain * one(*cut)
    return gain


def scatter_about(stream_key, extent, width, bound, cuts=(), kind=jnp.bfloat16):
    loudness = steps_of(stream_key, extent, cuts, -0.22, 0.18) if cuts else 1.0
    entries = jax.random.normal(stream_key, extent, jnp.float32) * width * loudness
    return jnp.minimum(jnp.maximum(entries, -bound), bound).astype(kind)


def setup_inputs(seed: int = 0, part: int = 0) -> dict:
    keys = jax.random.split(jax.random.key(seed), 8)
    part_keys = jax.random.split(jax.random.fold_in(keys[7], part), 8)
    initial_rates = scatter_about(part_keys[0], (B, NEURONS), 0.5, 3.0, ((1, 16),), jnp.float32)
    stimulus = scatter_about(part_keys[1], (STEPS, B, NEURONS), 0.5, 3.0, ((2, 16),))
    tile_values = scatter_about(keys[2], (DEVS * CAP, TILE, TILE), (TILE * CAP // (8 * OWN_T)) ** -0.5, 0.25, ((0, 16),))
    tile_rows = draw_tile_rows(jax.random.fold_in(keys[7], 71), part)
    tile_cols = draw_tile_cols(jax.random.fold_in(keys[7], 71), part)
    tile_count = draw_tile_count(jax.random.fold_in(keys[7], 71), part)
    cotangent = scatter_about(part_keys[6], (B, NEURONS), 1.0, 6.0, ((1, 16),), jnp.float32)
    return {"initial_rates": initial_rates, "stimulus": stimulus, "tile_values": tile_values, "tile_rows": tile_rows, "tile_cols": tile_cols, "tile_count": tile_count, "cotangent": cotangent}


step_ratio = 0.5


def slot_maps(tile_rows, tile_cols, tile_count):
    list_index = jnp.arange(DEVS, dtype=jnp.int32)
    col_block = list_index // N_ROW
    row_place = list_index % N_ROW
    out_tiles = (col_block[:, None] * RB + tile_rows).astype(jnp.int32)
    in_tiles = (((tile_cols // OWN_T) * N_ROW + row_place[:, None]) * OWN_T + tile_cols % OWN_T).astype(jnp.int32)
    live_mask = (jnp.arange(CAP, dtype=jnp.int32)[None, :] < tile_count[:, None]).astype(jnp.float32)
    return out_tiles, in_tiles, live_mask


def spread(values, out_tiles, in_tiles, live_mask, signal, forward):
    def per_list(running, carried):
        blocks, target, source, weight = carried
        if forward:
            picked = signal[:, source, :]
            products = jnp.einsum("bkc,koc->bko", picked, blocks.astype(jnp.float32), precision=lax.Precision.HIGHEST)
            return running.at[:, target, :].add(products * weight[None, :, None]), None
        picked = signal[:, target, :]
        products = jnp.einsum("bko,koc->bkc", picked, blocks.astype(jnp.float32), precision=lax.Precision.HIGHEST)
        return running.at[:, source, :].add(products * weight[None, :, None]), None

    running, _ = lax.scan(per_list, jnp.zeros_like(signal), (values, out_tiles, in_tiles, live_mask))
    return running


def reference(initial_rates, stimulus, tile_values, tile_rows, tile_cols, tile_count, cotangent):
    out_tiles, in_tiles, live_mask = slot_maps(tile_rows, tile_cols, tile_count)
    values = tile_values.reshape(DEVS, CAP, TILE, TILE)
    all_tiles = NEURONS // TILE
    rates = initial_rates.astype(jnp.float32)
    sent_list = []
    active_list = []
    for step_index in range(STEPS):
        sent_rates = rates.astype(jnp.bfloat16).astype(jnp.float32).reshape(B, all_tiles, TILE)
        current = spread(values, out_tiles, in_tiles, live_mask, sent_rates, True).reshape(B, NEURONS)
        active = jnp.tanh(current + stimulus[step_index].astype(jnp.float32))
        rates = rates + step_ratio * (active - rates)
        sent_list.append(sent_rates)
        active_list.append(active)
    adjoint = cotangent.astype(jnp.float32)
    delta_list = [None] * STEPS
    for step_index in reversed(range(STEPS)):
        delta = step_ratio * adjoint * (1.0 - active_list[step_index] ** 2)
        sent_delta = delta.astype(jnp.bfloat16).astype(jnp.float32).reshape(B, all_tiles, TILE)
        back = spread(values, out_tiles, in_tiles, live_mask, sent_delta, False).reshape(B, NEURONS)
        adjoint = step_ratio * adjoint + back
        delta_list[step_index] = sent_delta
    sent_stack = jnp.stack(sent_list)
    delta_stack = jnp.stack(delta_list)

    def list_gradient(carried):
        target, source, weight = carried
        left_part = delta_stack[:, :, target, :]
        right_part = sent_stack[:, :, source, :]
        summed = jnp.einsum("sbko,sbkc->koc", left_part, right_part, precision=lax.Precision.HIGHEST)
        return (summed * weight[:, None, None]).astype(jnp.bfloat16)

    gradient = lax.map(list_gradient, (out_tiles, in_tiles, live_mask))
    return rates, adjoint, gradient.reshape(DEVS * CAP, TILE, TILE)
```

```python
import jax
import jax.numpy as jnp
from jax import lax
from jax.experimental import pallas as pl
from jax.experimental.pallas import tpu as pltpu
from jax.sharding import PartitionSpec as P

STEPS = 3
MIB = 1 << 20

step_ratio = 0.5


def partner(value, axis, shift):
    size = lax.axis_size(axis)
    return lax.ppermute(value, axis, [(index, index ^ shift) for index in range(size)])


def gather_relative(value, axis):
    size = lax.axis_size(axis)
    received = {s: partner(value, axis, s) for s in reversed(range(1, size))}
    return [value] + [received[s] for s in range(1, size)]


def reduce_relative(pieces, axis):
    size = lax.axis_size(axis)
    received = {s: partner(pieces[s], axis, s) for s in reversed(range(1, size))}
    return [pieces[0]] + [received[s] for s in range(1, size)]


def in_vmem(count):
    return [pl.BlockSpec(memory_space=pltpu.VMEM)] * count


def in_smem(count):
    return [pl.BlockSpec(memory_space=pltpu.SMEM)] * count


def relative(tile, place, own_tiles):
    return ((tile // own_tiles) ^ place) * own_tiles + tile % own_tiles


def tile_slice(index, tile_width):
    return pl.ds(pl.multiple_of(index * tile_width, tile_width), tile_width)


def dense_weights(tile_values, rows, cols, count, row_width, col_width):
    slot_count, tile_width = tile_values.shape[:2]

    def kernel(rows_ref, cols_ref, count_ref, values_ref, dense_ref):
        dense_ref[...] = jnp.zeros_like(dense_ref)

        def one(slot, carry):
            dense_ref[
                tile_slice(rows_ref[slot], tile_width), tile_slice(cols_ref[slot], tile_width)
            ] = values_ref[slot]
            return carry

        lax.fori_loop(0, count_ref[0], one, 0)

    total = 2 * (slot_count * tile_width * tile_width + row_width * col_width)
    return pl.pallas_call(
        kernel,
        out_shape=jax.ShapeDtypeStruct((row_width, col_width), jnp.bfloat16),
        in_specs=in_smem(3) + in_vmem(1),
        out_specs=pl.BlockSpec(memory_space=pltpu.VMEM),
        compiler_params=pltpu.CompilerParams(vmem_limit_bytes=total + 4 * MIB),
    )(rows, cols, count, tile_values)


def multiply(blocks, dense, pieces, forward):
    batch, width = blocks[0].shape
    contract = (((1,), (1 if forward else 0,)), ((), ()))

    def kernel(*refs):
        dense_ref = refs[len(blocks)]
        outs = refs[len(blocks) + 1 :]
        whole = jnp.concatenate([ref[...] for ref in refs[: len(blocks)]], axis=1)
        for index, out in enumerate(outs):
            span = slice(index * width, (index + 1) * width)
            part = dense_ref[span, :] if forward else dense_ref[:, span]
            out[...] = lax.dot_general(
                whole, part, contract, preferred_element_type=jnp.float32
            ).astype(out.dtype)

    return pl.pallas_call(
        kernel,
        out_shape=[jax.ShapeDtypeStruct((batch, width), jnp.float32)]
        + [jax.ShapeDtypeStruct((batch, width), jnp.bfloat16)] * (pieces - 1),
        in_specs=in_vmem(len(blocks) + 1),
        out_specs=in_vmem(pieces),
        compiler_params=pltpu.CompilerParams(vmem_limit_bytes=2 * dense.size + 8 * MIB),
    )(*blocks, dense)


def tile_gradients(delta_blocks, sent_blocks, rows, cols, count, slot_count, tile_width):
    steps, batch, width = (len(delta_blocks), *delta_blocks[0][0].shape)
    row_parts, col_parts = len(delta_blocks[0]), len(sent_blocks[0])
    operands = [x for step in delta_blocks for x in step] + [x for step in sent_blocks for x in step]
    row_width, col_width = row_parts * width, col_parts * width

    def kernel(rows_ref, cols_ref, count_ref, *refs):
        inputs, out_ref, left, right = refs[: len(operands)], *refs[len(operands) :]
        position = 0
        for side, parts in ((left, row_parts), (right, col_parts)):
            for step in range(steps):
                for part in range(parts):
                    side[step * batch : (step + 1) * batch, part * width : (part + 1) * width] = inputs[
                        position
                    ][...]
                    position += 1

        def one(slot, carry):
            live = slot < count_ref[0]

            @pl.when(live)
            def _():
                out_ref[slot] = lax.dot_general(
                    left[:, tile_slice(rows_ref[slot], tile_width)],
                    right[:, tile_slice(cols_ref[slot], tile_width)],
                    (((0,), (0,)), ((), ())),
                    preferred_element_type=jnp.float32,
                ).astype(jnp.bfloat16)

            @pl.when(jnp.logical_not(live))
            def _():
                out_ref[slot] = jnp.zeros((tile_width, tile_width), jnp.bfloat16)

            return carry

        lax.fori_loop(0, slot_count, one, 0)

    total = 2 * slot_count * tile_width * tile_width + 8 * steps * batch * (row_width + col_width)
    return pl.pallas_call(
        kernel,
        out_shape=jax.ShapeDtypeStruct((slot_count, tile_width, tile_width), jnp.bfloat16),
        in_specs=in_smem(3) + in_vmem(len(operands)),
        out_specs=pl.BlockSpec(memory_space=pltpu.VMEM),
        scratch_shapes=[
            pltpu.VMEM((steps * batch, row_width), jnp.bfloat16),
            pltpu.VMEM((steps * batch, col_width), jnp.bfloat16),
        ],
        compiler_params=pltpu.CompilerParams(vmem_limit_bytes=total + 8 * MIB),
    )(rows, cols, count, *operands)


def total_of(parts):
    total = parts[0].astype(jnp.float32)
    for part in parts[1:]:
        total = total + part.astype(jnp.float32)
    return total


def body(initial_rates, stimulus, tile_values, tile_rows, tile_cols, tile_count, cotangent):
    slot_count, tile_width = tile_values.shape[:2]
    owned_width = initial_rates.shape[1]
    own_tiles = owned_width // tile_width
    row_parts, col_parts = lax.axis_size("row"), lax.axis_size("col")
    rows = relative(tile_rows[0], lax.axis_index("row"), own_tiles)
    cols = relative(tile_cols[0], lax.axis_index("col"), own_tiles)
    dense = dense_weights(
        tile_values, rows, cols, tile_count, row_parts * owned_width, col_parts * owned_width
    )
    rates = initial_rates
    sent_list = []
    active_list = []
    for step_index in range(STEPS):
        sent = gather_relative(rates.astype(jnp.bfloat16), "col")
        pieces = multiply(sent, dense, row_parts, True)
        current = total_of(reduce_relative(pieces, "row"))
        active = jnp.tanh(current + stimulus[step_index].astype(jnp.float32))
        rates = rates + step_ratio * (active - rates)
        sent_list.append(sent)
        active_list.append(active)
    adjoint = cotangent
    delta_list = [None] * STEPS
    for step_index in reversed(range(STEPS)):
        delta = step_ratio * adjoint * (1.0 - active_list[step_index] ** 2)
        chosen = gather_relative(delta.astype(jnp.bfloat16), "row")
        pieces = multiply(chosen, dense, col_parts, False)
        adjoint = step_ratio * adjoint + total_of(reduce_relative(pieces, "col"))
        delta_list[step_index] = chosen
    gradient = tile_gradients(
        delta_list, sent_list, rows, cols, tile_count, slot_count, tile_width
    )
    return (rates, adjoint, gradient)


def solution(mesh):
    return jax.shard_map(
        body,
        mesh=mesh,
        in_specs=(
            P("group", ("col", "row")),
            P(None, "group", ("col", "row")),
            P(("col", "row"), None, None),
            P(("col", "row"), None),
            P(("col", "row"), None),
            P(("col", "row")),
            P("group", ("col", "row")),
        ),
        out_specs=(
            P("group", ("col", "row")),
            P("group", ("col", "row")),
            P(("group", "col", "row"), None, None),
        ),
        check_vma=False,
    )
```

```python
import jax
import jax.numpy as jnp
from jax import lax
from jax.experimental import pallas as pl
from jax.experimental.pallas import tpu as pltpu
from jax.sharding import PartitionSpec as P

STEPS = 3
MIB = 1 << 20

step_ratio = 0.5


def partner(value, axis, shift):
    size = lax.axis_size(axis)
    return lax.ppermute(value, axis, [(index, index ^ shift) for index in range(size)])


def gather_relative(value, axis):
    size = lax.axis_size(axis)
    received = {s: partner(value, axis, s) for s in reversed(range(1, size))}
    return [value] + [received[s] for s in range(1, size)]


def reduce_relative(pieces, axis):
    size = lax.axis_size(axis)
    received = {s: partner(pieces[s], axis, s) for s in range(1, size)}
    return [pieces[0]] + [received[s] for s in range(1, size)]


def in_vmem(count):
    return [pl.BlockSpec(memory_space=pltpu.VMEM)] * count


def in_smem(count):
    return [pl.BlockSpec(memory_space=pltpu.SMEM)] * count


def relative(tile, place, own_tiles):
    return ((tile // own_tiles) ^ place) * own_tiles + tile % own_tiles


def tile_slice(index, tile_width):
    return pl.ds(pl.multiple_of(index * tile_width, tile_width), tile_width)


def dense_weights(tile_values, rows, cols, count, row_width, col_width):
    slot_count, tile_width = tile_values.shape[:2]

    def kernel(rows_ref, cols_ref, count_ref, values_ref, dense_ref, sems):
        dense_ref[...] = jnp.zeros_like(dense_ref)

        def copy(slot):
            place = dense_ref.at[
                tile_slice(rows_ref[slot], tile_width), tile_slice(cols_ref[slot], tile_width)
            ]
            return pltpu.make_async_copy(values_ref.at[slot], place, sems.at[slot])

        def start(slot, carry):
            copy(slot).start()
            return carry

        def wait(slot, carry):
            copy(slot).wait()
            return carry

        lax.fori_loop(0, count_ref[0], start, 0)
        lax.fori_loop(0, count_ref[0], wait, 0)

    return pl.pallas_call(
        kernel,
        out_shape=jax.ShapeDtypeStruct((row_width, col_width), jnp.bfloat16),
        in_specs=in_smem(3) + [pl.BlockSpec(memory_space=pltpu.HBM)],
        out_specs=pl.BlockSpec(memory_space=pltpu.VMEM),
        scratch_shapes=[pltpu.SemaphoreType.DMA((slot_count,))],
        compiler_params=pltpu.CompilerParams(
            vmem_limit_bytes=2 * row_width * col_width + 4 * MIB
        ),
    )(rows, cols, count, tile_values)


def multiply(blocks, dense, pieces, forward):
    batch, width = blocks[0].shape
    contract = (((1,), (1 if forward else 0,)), ((), ()))

    def kernel(*refs):
        dense_ref = refs[len(blocks)]
        outs = refs[len(blocks) + 1 :]
        whole = jnp.concatenate(
            [ref[...].astype(jnp.bfloat16) for ref in refs[: len(blocks)]], axis=1
        )
        for index, out in enumerate(outs):
            span = slice(index * width, (index + 1) * width)
            part = dense_ref[span, :] if forward else dense_ref[:, span]
            out[...] = lax.dot_general(
                whole, part, contract, preferred_element_type=jnp.float32
            ).astype(out.dtype)

    return pl.pallas_call(
        kernel,
        out_shape=[jax.ShapeDtypeStruct((batch, width), jnp.float32)]
        + [jax.ShapeDtypeStruct((batch, width), jnp.bfloat16)] * (pieces - 1),
        in_specs=in_vmem(len(blocks) + 1),
        out_specs=in_vmem(pieces),
        compiler_params=pltpu.CompilerParams(vmem_limit_bytes=2 * dense.size + 8 * MIB),
    )(*blocks, dense)


def tile_gradients(delta_blocks, sent_blocks, rows, cols, count, slot_count, tile_width):
    steps, batch, width = (len(delta_blocks), *delta_blocks[0][0].shape)
    row_parts, col_parts = len(delta_blocks[0]), len(sent_blocks[0])
    operands = [x for step in delta_blocks for x in step] + [x for step in sent_blocks for x in step]
    row_width, col_width = row_parts * width, col_parts * width

    def kernel(rows_ref, cols_ref, count_ref, *refs):
        inputs, out_ref = refs[: len(operands)], refs[len(operands)]
        left, right, dense, empty, sems = refs[len(operands) + 1 :]
        position = 0
        for side, parts in ((left, row_parts), (right, col_parts)):
            for step in range(steps):
                for part in range(parts):
                    side[
                        step * batch : (step + 1) * batch, part * width : (part + 1) * width
                    ] = inputs[position][...].astype(jnp.bfloat16)
                    position += 1
        empty[...] = jnp.zeros_like(empty)
        for part in range(row_parts):
            span = slice(part * width, (part + 1) * width)
            dense[span, :] = lax.dot_general(
                left[:, span],
                right[...],
                (((0,), (0,)), ((), ())),
                preferred_element_type=jnp.float32,
            ).astype(jnp.bfloat16)

        def product(slot):
            place = dense.at[
                tile_slice(rows_ref[slot], tile_width), tile_slice(cols_ref[slot], tile_width)
            ]
            return pltpu.make_async_copy(place, out_ref.at[slot], sems.at[slot])

        def nothing(slot):
            return pltpu.make_async_copy(empty, out_ref.at[slot], sems.at[slot])

        def each(first, last, act):
            def one(slot, carry):
                act(slot)
                return carry

            lax.fori_loop(first, last, one, 0)

        live = count_ref[0]
        each(0, live, lambda slot: product(slot).start())
        each(live, slot_count, lambda slot: nothing(slot).start())
        each(0, live, lambda slot: product(slot).wait())
        each(live, slot_count, lambda slot: nothing(slot).wait())

    total = 2 * row_width * col_width + 8 * steps * batch * (row_width + col_width)
    total += 4 * width * col_width
    return pl.pallas_call(
        kernel,
        out_shape=jax.ShapeDtypeStruct((slot_count, tile_width, tile_width), jnp.bfloat16),
        in_specs=in_smem(3) + in_vmem(len(operands)),
        out_specs=pl.BlockSpec(memory_space=pltpu.HBM),
        scratch_shapes=[
            pltpu.VMEM((steps * batch, row_width), jnp.bfloat16),
            pltpu.VMEM((steps * batch, col_width), jnp.bfloat16),
            pltpu.VMEM((row_width, col_width), jnp.bfloat16),
            pltpu.VMEM((tile_width, tile_width), jnp.bfloat16),
            pltpu.SemaphoreType.DMA((slot_count,)),
        ],
        compiler_params=pltpu.CompilerParams(vmem_limit_bytes=total + 8 * MIB),
    )(rows, cols, count, *operands)


def total_of(parts):
    total = parts[0].astype(jnp.float32)
    for part in reversed(parts[1:]):
        total = total + part.astype(jnp.float32)
    return total


def body(initial_rates, stimulus, tile_values, tile_rows, tile_cols, tile_count, cotangent):
    slot_count, tile_width = tile_values.shape[:2]
    owned_width = initial_rates.shape[1]
    own_tiles = owned_width // tile_width
    row_parts, col_parts = lax.axis_size("row"), lax.axis_size("col")
    rows = relative(tile_rows[0], lax.axis_index("row"), own_tiles)
    cols = relative(tile_cols[0], lax.axis_index("col"), own_tiles)
    dense = dense_weights(
        tile_values, rows, cols, tile_count, row_parts * owned_width, col_parts * owned_width
    )
    rates = initial_rates
    sent_list = []
    active_list = []
    for step_index in range(STEPS):
        sent = gather_relative(rates if step_index == 0 else rates.astype(jnp.bfloat16), "col")
        pieces = multiply(sent, dense, row_parts, True)
        current = total_of(reduce_relative(pieces, "row"))
        active = jnp.tanh(current + stimulus[step_index].astype(jnp.float32))
        rates = rates + step_ratio * (active - rates)
        sent_list.append(sent)
        active_list.append(active)
    adjoint = cotangent
    delta_list = [None] * STEPS
    for step_index in reversed(range(STEPS)):
        delta = step_ratio * adjoint * (1.0 - active_list[step_index] ** 2)
        chosen = gather_relative(delta.astype(jnp.bfloat16), "row")
        pieces = multiply(chosen, dense, col_parts, False)
        adjoint = step_ratio * adjoint + total_of(reduce_relative(pieces, "col"))
        delta_list[step_index] = chosen
    gradient = tile_gradients(
        delta_list, sent_list, rows, cols, tile_count, slot_count, tile_width
    )
    return (rates, adjoint, gradient)


def solution(mesh):
    return jax.shard_map(
        body,
        mesh=mesh,
        in_specs=(
            P("group", ("col", "row")),
            P(None, "group", ("col", "row")),
            P(("col", "row"), None, None),
            P(("col", "row"), None),
            P(("col", "row"), None),
            P(("col", "row")),
            P("group", ("col", "row")),
        ),
        out_specs=(
            P("group", ("col", "row")),
            P("group", ("col", "row")),
            P(("group", "col", "row"), None, None),
        ),
        check_vma=False,
    )
```

```python
import math

import jax
import jax.numpy as jnp
from jax import lax
from jax.experimental import pallas as pl
from jax.experimental.pallas import tpu as pltpu
from jax.sharding import PartitionSpec as P

STEPS = 3
MIB = 1 << 20

step_ratio = 0.5


def partner(value, axis, shift):
    size = lax.axis_size(axis)
    return lax.ppermute(value, axis, [(index, index ^ shift) for index in range(size)])


def gather_relative(value, axis):
    size = lax.axis_size(axis)
    received = {s: partner(value, axis, s) for s in reversed(range(1, size))}
    return [value] + [received[s] for s in range(1, size)]


def reduce_relative(pieces, axis):
    size = lax.axis_size(axis)
    received = {s: partner(pieces[s], axis, s) for s in range(1, size)}
    return [pieces[0]] + [received[s] for s in range(1, size)]


def in_vmem(count):
    return [pl.BlockSpec(memory_space=pltpu.VMEM)] * count


def in_smem(count):
    return [pl.BlockSpec(memory_space=pltpu.SMEM)] * count


def relative(tile, place, own_tiles):
    return lax.bitwise_xor(tile, place * own_tiles)


def tile_slice(index, tile_width):
    return pl.ds(pl.multiple_of(index * tile_width, tile_width), tile_width)


def slot_place(rows_ref, cols_ref, own_tiles, tile_width):
    row_place, col_place = lax.axis_index("row"), lax.axis_index("col")

    def place(slot):
        row = relative(rows_ref[0, slot], row_place, own_tiles)
        col = relative(cols_ref[0, slot], col_place, own_tiles)
        return tile_slice(row, tile_width), tile_slice(col, tile_width)

    return place


def in_hbm(value):
    return pltpu.with_memory_space_constraint(value, pltpu.HBM)


def index_copies(rows_hbm, cols_hbm, rows_ref, cols_ref, sems):
    return [
        pltpu.make_async_copy(rows_hbm, rows_ref, sems.at[0]),
        pltpu.make_async_copy(cols_hbm, cols_ref, sems.at[1]),
    ]


def dense_weights(tile_values, rows, cols, count, own_tiles, row_width, col_width):
    slot_count, tile_width = tile_values.shape[:2]
    chunk = slot_count // math.gcd(slot_count, 8)

    def kernel(count_ref, rows_hbm, cols_hbm, values_hbm, dense_ref, *scratch):
        values, rows_ref, cols_ref, value_sems, index_sems = scratch
        indices = index_copies(rows_hbm, cols_hbm, rows_ref, cols_ref, index_sems)
        loads = [
            pltpu.make_async_copy(
                values_hbm.at[first : first + chunk],
                values.at[first : first + chunk],
                value_sems.at[first // chunk],
            )
            for first in range(0, slot_count, chunk)
        ]
        for copy in indices + loads:
            copy.start()
        dense_ref[...] = jnp.zeros_like(dense_ref)
        for copy in indices:
            copy.wait()
        place = slot_place(rows_ref, cols_ref, own_tiles, tile_width)

        def store(slot, carry):
            dense_ref[place(slot)] = values[slot]
            return carry

        for number, copy in enumerate(loads):
            copy.wait()
            first = number * chunk
            last = jnp.clip(count_ref[0], first, first + chunk)
            lax.fori_loop(first, last, store, 0)

    return pl.pallas_call(
        kernel,
        out_shape=jax.ShapeDtypeStruct((row_width, col_width), jnp.bfloat16),
        in_specs=in_smem(1) + [pl.BlockSpec(memory_space=pltpu.HBM)] * 3,
        out_specs=pl.BlockSpec(memory_space=pltpu.VMEM),
        scratch_shapes=[
            pltpu.VMEM(tile_values.shape, tile_values.dtype),
            pltpu.SMEM(rows.shape, rows.dtype),
            pltpu.SMEM(cols.shape, cols.dtype),
            pltpu.SemaphoreType.DMA((slot_count // chunk,)),
            pltpu.SemaphoreType.DMA((2,)),
        ],
        compiler_params=pltpu.CompilerParams(
            vmem_limit_bytes=2 * (row_width * col_width + tile_values.size) + 4 * MIB
        ),
    )(count, in_hbm(rows), in_hbm(cols), in_hbm(tile_values))


def multiply(blocks, dense, pieces, forward):
    batch, width = blocks[0].shape
    contract = (((1,), (1 if forward else 0,)), ((), ()))

    def kernel(*refs):
        dense_ref = refs[len(blocks)]
        outs = refs[len(blocks) + 1 :]
        whole = jnp.concatenate(
            [ref[...].astype(jnp.bfloat16) for ref in refs[: len(blocks)]], axis=1
        )
        for index, out in enumerate(outs):
            span = slice(index * width, (index + 1) * width)
            part = dense_ref[span, :] if forward else dense_ref[:, span]
            out[...] = lax.dot_general(
                whole, part, contract, preferred_element_type=jnp.float32
            ).astype(out.dtype)

    return pl.pallas_call(
        kernel,
        out_shape=[jax.ShapeDtypeStruct((batch, width), jnp.float32)]
        + [jax.ShapeDtypeStruct((batch, width), jnp.bfloat16)] * (pieces - 1),
        in_specs=in_vmem(len(blocks) + 1),
        out_specs=in_vmem(pieces),
        compiler_params=pltpu.CompilerParams(vmem_limit_bytes=2 * dense.size + 8 * MIB),
    )(*blocks, dense)


def last_outputs(
    delta_blocks, sent_blocks, rows, cols, count, rates, active, slot_count, own_tiles
):
    steps, batch, width = (len(delta_blocks), *delta_blocks[0][0].shape)
    tile_width = width // own_tiles
    row_parts, col_parts = len(delta_blocks[0]), len(sent_blocks[0])
    operands = [x for step in delta_blocks for x in step] + [x for step in sent_blocks for x in step]
    row_width, col_width = row_parts * width, col_parts * width

    def kernel(count_ref, rows_hbm, cols_hbm, *refs):
        inputs = refs[: len(operands)]
        rates_ref, active_ref, out_ref, last_rates_ref = refs[len(operands) : len(operands) + 4]
        rows_ref, cols_ref, left, right, dense, empty, last_rates, index_sems, out_sem, rate_sem = (
            refs[len(operands) + 4 :]
        )
        indices = index_copies(rows_hbm, cols_hbm, rows_ref, cols_ref, index_sems)
        for copy in indices:
            copy.start()
        last_rates[...] = rates_ref[...] + step_ratio * (active_ref[...] - rates_ref[...])
        rate_copy = pltpu.make_async_copy(last_rates, last_rates_ref, rate_sem)
        rate_copy.start()
        empty[...] = jnp.zeros_like(empty)
        position = 0
        for side, parts in ((left, row_parts), (right, col_parts)):
            for step in range(steps):
                for part in range(parts):
                    side[
                        step * batch : (step + 1) * batch, part * width : (part + 1) * width
                    ] = inputs[position][...].astype(jnp.bfloat16)
                    position += 1
        for part in range(row_parts):
            span = slice(part * width, (part + 1) * width)
            dense[span, :] = lax.dot_general(
                left[:, span],
                right[...],
                (((0,), (0,)), ((), ())),
                preferred_element_type=jnp.float32,
            ).astype(jnp.bfloat16)
        for copy in indices:
            copy.wait()
        place = slot_place(rows_ref, cols_ref, own_tiles, tile_width)

        def live(slot, carry):
            pltpu.make_async_copy(dense.at[place(slot)], out_ref.at[slot], out_sem).start()
            return carry

        def dead(slot, carry):
            pltpu.make_async_copy(empty, out_ref.at[slot], out_sem).start()
            return carry

        lax.fori_loop(0, count_ref[0], live, 0)
        lax.fori_loop(count_ref[0], slot_count, dead, 0)
        rate_copy.wait()
        pltpu.make_async_copy(out_ref, out_ref, out_sem).wait()

    total = 2 * row_width * col_width + 8 * steps * batch * (row_width + col_width)
    total += 4 * width * col_width
    return pl.pallas_call(
        kernel,
        out_shape=[
            jax.ShapeDtypeStruct((slot_count, tile_width, tile_width), jnp.bfloat16),
            jax.ShapeDtypeStruct(rates.shape, jnp.float32),
        ],
        in_specs=in_smem(1)
        + [pl.BlockSpec(memory_space=pltpu.HBM)] * 2
        + in_vmem(len(operands) + 2),
        out_specs=[pl.BlockSpec(memory_space=pltpu.HBM)] * 2,
        scratch_shapes=[
            pltpu.SMEM(rows.shape, rows.dtype),
            pltpu.SMEM(cols.shape, cols.dtype),
            pltpu.VMEM((steps * batch, row_width), jnp.bfloat16),
            pltpu.VMEM((steps * batch, col_width), jnp.bfloat16),
            pltpu.VMEM((row_width, col_width), jnp.bfloat16),
            pltpu.VMEM((tile_width, tile_width), jnp.bfloat16),
            pltpu.VMEM(rates.shape, jnp.float32),
            pltpu.SemaphoreType.DMA((2,)),
            pltpu.SemaphoreType.DMA,
            pltpu.SemaphoreType.DMA,
        ],
        compiler_params=pltpu.CompilerParams(vmem_limit_bytes=total + 8 * MIB),
    )(count, in_hbm(rows), in_hbm(cols), *operands, rates, active)


def total_of(parts):
    total = parts[0].astype(jnp.float32)
    for part in reversed(parts[1:]):
        total = total + part.astype(jnp.float32)
    return total


def body(initial_rates, stimulus, tile_values, tile_rows, tile_cols, tile_count, cotangent):
    slot_count, tile_width = tile_values.shape[:2]
    owned_width = initial_rates.shape[1]
    own_tiles = owned_width // tile_width
    row_parts, col_parts = lax.axis_size("row"), lax.axis_size("col")
    dense = dense_weights(
        tile_values,
        tile_rows,
        tile_cols,
        tile_count,
        own_tiles,
        row_parts * owned_width,
        col_parts * owned_width,
    )
    rates = initial_rates
    sent_list = []
    active_list = []
    for step_index in range(STEPS):
        if step_index:
            rates = rates + step_ratio * (active_list[-1] - rates)
        sent = gather_relative(rates.astype(jnp.bfloat16) if step_index else rates, "col")
        pieces = multiply(sent, dense, row_parts, True)
        current = total_of(reduce_relative(pieces, "row"))
        active_list.append(jnp.tanh(current + stimulus[step_index].astype(jnp.float32)))
        sent_list.append(sent)
    adjoint = cotangent
    terms = []
    delta_list = [None] * STEPS
    for step_index in reversed(range(STEPS)):
        if terms:
            adjoint = step_ratio * adjoint + total_of(terms)
        delta = step_ratio * adjoint * (1.0 - active_list[step_index] ** 2)
        chosen = gather_relative(delta.astype(jnp.bfloat16), "row")
        pieces = multiply(chosen, dense, col_parts, False)
        terms = reduce_relative(pieces, "col")
        delta_list[step_index] = chosen
    gradient, rates = last_outputs(
        delta_list,
        sent_list,
        tile_rows,
        tile_cols,
        tile_count,
        rates,
        active_list[-1],
        slot_count,
        own_tiles,
    )
    adjoint = step_ratio * adjoint + total_of(terms)
    return (rates, adjoint, gradient)


def solution(mesh):
    return jax.shard_map(
        body,
        mesh=mesh,
        in_specs=(
            P("group", ("col", "row")),
            P(None, "group", ("col", "row")),
            P(("col", "row"), None, None),
            P(("col", "row"), None),
            P(("col", "row"), None),
            P(("col", "row")),
            P("group", ("col", "row")),
        ),
        out_specs=(
            P("group", ("col", "row")),
            P("group", ("col", "row")),
            P(("group", "col", "row"), None, None),
        ),
        check_vma=False,
    )
```

```python
import math

import jax
import jax.numpy as jnp
from jax import lax
from jax.experimental import pallas as pl
from jax.experimental.pallas import tpu as pltpu
from jax.sharding import PartitionSpec as P

STEPS = 3
TWIN = 2
MIB = 1 << 20

step_ratio = 0.5


def partner(value, axis, shift):
    size = lax.axis_size(axis)
    return lax.ppermute(value, axis, [(index, index ^ shift) for index in range(size)])


def gather_relative(value, axis):
    size = lax.axis_size(axis)
    received = {s: partner(value, axis, s) for s in reversed(range(1, size))}
    return [value] + [received[s] for s in range(1, size)]


def reduce_relative(pieces, axis):
    size = lax.axis_size(axis)
    received = {s: partner(pieces[s], axis, s) for s in range(1, size)}
    return [pieces[0]] + [received[s] for s in range(1, size)]


def in_vmem(count):
    return [pl.BlockSpec(memory_space=pltpu.VMEM)] * count


def in_smem(count):
    return [pl.BlockSpec(memory_space=pltpu.SMEM)] * count


def relative(tile, place, own_tiles):
    return lax.bitwise_xor(tile, place * own_tiles)


def tile_slice(index, tile_width):
    return pl.ds(pl.multiple_of(index * tile_width, tile_width), tile_width)


def slot_place(rows_ref, cols_ref, own_tiles, tile_width):
    row_place, col_place = lax.axis_index("row"), lax.axis_index("col")

    def place(slot):
        row = relative(rows_ref[0, slot], row_place, own_tiles)
        col = relative(cols_ref[0, slot], col_place, own_tiles)
        return tile_slice(row, tile_width), tile_slice(col, tile_width)

    return place


def in_hbm(value):
    return pltpu.with_memory_space_constraint(value, pltpu.HBM)


def index_copies(rows_hbm, cols_hbm, rows_ref, cols_ref, sems):
    return [
        pltpu.make_async_copy(rows_hbm, rows_ref, sems.at[0]),
        pltpu.make_async_copy(cols_hbm, cols_ref, sems.at[1]),
    ]


def dense_weights(tile_values, rows, cols, count, own_tiles, row_width, col_width):
    slot_count, tile_width = tile_values.shape[:2]
    chunk = slot_count // math.gcd(slot_count, 8)

    def kernel(count_ref, rows_hbm, cols_hbm, values_hbm, dense_ref, *scratch):
        values, rows_ref, cols_ref, value_sems, index_sems = scratch
        indices = index_copies(rows_hbm, cols_hbm, rows_ref, cols_ref, index_sems)
        loads = [
            pltpu.make_async_copy(
                values_hbm.at[first : first + chunk],
                values.at[first : first + chunk],
                value_sems.at[first // chunk],
            )
            for first in range(0, slot_count, chunk)
        ]
        for copy in indices + loads:
            copy.start()
        dense_ref[...] = jnp.zeros_like(dense_ref)
        for copy in indices:
            copy.wait()
        place = slot_place(rows_ref, cols_ref, own_tiles, tile_width)

        def store(slot, carry):
            dense_ref[place(slot)] = values[slot]
            return carry

        for number, copy in enumerate(loads):
            copy.wait()
            first = number * chunk
            last = jnp.clip(count_ref[0], first, first + chunk)
            lax.fori_loop(first, last, store, 0)

    return pl.pallas_call(
        kernel,
        out_shape=jax.ShapeDtypeStruct((row_width, col_width), jnp.bfloat16),
        in_specs=in_smem(1) + [pl.BlockSpec(memory_space=pltpu.HBM)] * 3,
        out_specs=pl.BlockSpec(memory_space=pltpu.VMEM),
        scratch_shapes=[
            pltpu.VMEM(tile_values.shape, tile_values.dtype),
            pltpu.SMEM(rows.shape, rows.dtype),
            pltpu.SMEM(cols.shape, cols.dtype),
            pltpu.SemaphoreType.DMA((slot_count // chunk,)),
            pltpu.SemaphoreType.DMA((2,)),
        ],
        compiler_params=pltpu.CompilerParams(
            vmem_limit_bytes=2 * (row_width * col_width + tile_values.size) + 4 * MIB
        ),
    )(count, in_hbm(rows), in_hbm(cols), in_hbm(tile_values))


def start_order(axis):
    size = lax.axis_size(axis)
    far = [2, 3, 1] if axis == "row" else [3, 2, 1]
    return [s for s in range(size - 1, 3, -1)] + [s for s in far if s < size]


def transposed(dense):
    def kernel(dense_ref, out_ref):
        out_ref[...] = dense_ref[...].T

    return pl.pallas_call(
        kernel,
        out_shape=jax.ShapeDtypeStruct(dense.shape[::-1], dense.dtype),
        in_specs=in_vmem(1),
        out_specs=pl.BlockSpec(memory_space=pltpu.VMEM),
        compiler_params=pltpu.CompilerParams(vmem_limit_bytes=8 * dense.size + 8 * MIB),
        cost_estimate=pl.CostEstimate(
            flops=0, bytes_accessed=4 * dense.size, transcendentals=0
        ),
    )(dense)


def multiply(blocks, order, dense, axis, cuts, rider=None, stimulus=None):
    batch, width = (order[0].shape[0], dense.shape[axis] // len(blocks))
    out_width = dense.shape[1 - axis]
    contract = (((1,), (axis,)), ((), ()))
    extras = [x for x in (rider[1] if rider else None, stimulus) if x is not None]

    def kernel(*refs):
        dense_ref = refs[len(order)]
        outs = refs[len(order) + 1 + len(extras) :]
        parts = []
        for array, column in blocks:
            ref = refs[[x is array for x in order].index(True)]
            parts.append(ref[:, column * width : (column + 1) * width].astype(jnp.bfloat16))
        whole = jnp.concatenate(parts, axis=1)
        pieces = {}
        for index in range(out_width // width):
            span = slice(index * width, (index + 1) * width)
            part = dense_ref[:, span] if axis == 0 else dense_ref[span, :]
            pieces[index] = lax.dot_general(
                whole, part, contract, preferred_element_type=jnp.float32
            )
        if stimulus is not None:
            pieces[0] = pieces[0] + refs[len(order) + len(extras)][...].astype(jnp.float32)
        for number, (cut, out) in enumerate(zip(cuts, outs)):
            for place, index in enumerate(cut):
                span = slice(place * width, (place + 1) * width)
                out[:batch, span] = pieces[index].astype(out.dtype)
            if rider and rider[0] == number:
                out[batch:, :] = refs[len(order) + 1][...].astype(out.dtype)

    out_shape = []
    for number, cut in enumerate(cuts):
        rows = 2 * batch if rider and rider[0] == number else batch
        kind = jnp.bfloat16 if number else jnp.float32
        out_shape.append(jax.ShapeDtypeStruct((rows, len(cut) * width), kind))
    return pl.pallas_call(
        kernel,
        out_shape=out_shape,
        in_specs=in_vmem(len(order) + 1 + len(extras)),
        out_specs=in_vmem(len(out_shape)),
        compiler_params=pltpu.CompilerParams(vmem_limit_bytes=2 * dense.size + 8 * MIB),
        cost_estimate=pl.CostEstimate(
            flops=2 * batch * dense.size, bytes_accessed=2 * dense.size, transcendentals=0
        ),
    )(*order, dense, *extras)


def turn(kept, received, cotangent, rider):
    batch, width = cotangent.shape

    def kernel(*refs):
        kept_ref, cotangent_ref, rider_ref, active_ref, delta_ref = refs[len(received) :]
        current = kept_ref[...]
        for ref in refs[: len(received)]:
            current = current + ref[...].astype(jnp.float32)
        active = jnp.tanh(current)
        slope = step_ratio * (1.0 - active**2)
        active_ref[...] = active[:, :width]
        delta_ref[:, :width] = (cotangent_ref[...] * slope[:, :width]).astype(jnp.bfloat16)
        there = rider_ref[batch:, :].astype(jnp.float32)
        delta_ref[:, width:] = (there * slope[:, width:]).astype(jnp.bfloat16)

    return pl.pallas_call(
        kernel,
        out_shape=[
            jax.ShapeDtypeStruct((batch, width), jnp.float32),
            jax.ShapeDtypeStruct((batch, 2 * width), jnp.bfloat16),
        ],
        in_specs=in_vmem(len(received) + 3),
        out_specs=in_vmem(2),
        compiler_params=pltpu.CompilerParams(vmem_limit_bytes=8 * MIB),
        cost_estimate=pl.CostEstimate(
            flops=16 * batch * width,
            bytes_accessed=16 * batch * width,
            transcendentals=2 * batch * width,
        ),
    )(*received, kept, cotangent, rider)


def last_outputs(
    delta_blocks, sent_blocks, rows, cols, count, rates, active, slot_count, own_tiles
):
    steps, (batch, width) = len(delta_blocks), rates.shape
    tile_width = width // own_tiles
    row_parts, col_parts = len(delta_blocks[0]), len(sent_blocks[0])
    operands = []
    for step in delta_blocks + sent_blocks:
        for array, _ in step:
            if not any(array is x for x in operands):
                operands.append(array)
    row_width, col_width = row_parts * width, col_parts * width

    def stack(side, blocks, inputs):
        for step, parts in enumerate(blocks):
            for part, (array, column) in enumerate(parts):
                ref = inputs[[x is array for x in operands].index(True)]
                side[
                    step * batch : (step + 1) * batch, part * width : (part + 1) * width
                ] = ref[:, column * width : (column + 1) * width].astype(jnp.bfloat16)

    def kernel(count_ref, rows_hbm, cols_hbm, *refs):
        inputs = refs[: len(operands)]
        rates_ref, active_ref, out_ref, last_rates_ref = refs[len(operands) : len(operands) + 4]
        rows_ref, cols_ref, left, right, dense, empty, last_rates, index_sems, out_sem, rate_sem = (
            refs[len(operands) + 4 :]
        )
        indices = index_copies(rows_hbm, cols_hbm, rows_ref, cols_ref, index_sems)
        for copy in indices:
            copy.start()
        last_rates[...] = rates_ref[...] + step_ratio * (active_ref[...] - rates_ref[...])
        rate_copy = pltpu.make_async_copy(last_rates, last_rates_ref, rate_sem)
        rate_copy.start()
        empty[...] = jnp.zeros_like(empty)
        stack(left, delta_blocks, inputs)
        stack(right, sent_blocks, inputs)
        for part in range(row_parts):
            span = slice(part * width, (part + 1) * width)
            dense[span, :] = lax.dot_general(
                left[:, span],
                right[...],
                (((0,), (0,)), ((), ())),
                preferred_element_type=jnp.float32,
            ).astype(jnp.bfloat16)
        for copy in indices:
            copy.wait()
        place = slot_place(rows_ref, cols_ref, own_tiles, tile_width)

        def live(slot, carry):
            pltpu.make_async_copy(dense.at[place(slot)], out_ref.at[slot], out_sem).start()
            return carry

        def dead(slot, carry):
            pltpu.make_async_copy(empty, out_ref.at[slot], out_sem).start()
            return carry

        lax.fori_loop(0, count_ref[0], live, 0)
        lax.fori_loop(count_ref[0], slot_count, dead, 0)
        rate_copy.wait()
        pltpu.make_async_copy(out_ref, out_ref, out_sem).wait()

    total = 2 * row_width * col_width + 8 * steps * batch * (row_width + col_width)
    total += 4 * width * col_width
    return pl.pallas_call(
        kernel,
        out_shape=[
            jax.ShapeDtypeStruct((slot_count, tile_width, tile_width), jnp.bfloat16),
            jax.ShapeDtypeStruct(rates.shape, jnp.float32),
        ],
        in_specs=in_smem(1)
        + [pl.BlockSpec(memory_space=pltpu.HBM)] * 2
        + in_vmem(len(operands) + 2),
        out_specs=[pl.BlockSpec(memory_space=pltpu.HBM)] * 2,
        scratch_shapes=[
            pltpu.SMEM(rows.shape, rows.dtype),
            pltpu.SMEM(cols.shape, cols.dtype),
            pltpu.VMEM((steps * batch, row_width), jnp.bfloat16),
            pltpu.VMEM((steps * batch, col_width), jnp.bfloat16),
            pltpu.VMEM((row_width, col_width), jnp.bfloat16),
            pltpu.VMEM((tile_width, tile_width), jnp.bfloat16),
            pltpu.VMEM(rates.shape, jnp.float32),
            pltpu.SemaphoreType.DMA((2,)),
            pltpu.SemaphoreType.DMA,
            pltpu.SemaphoreType.DMA,
        ],
        compiler_params=pltpu.CompilerParams(vmem_limit_bytes=total + 8 * MIB),
    )(count, in_hbm(rows), in_hbm(cols), *operands, rates, active)


def total_of(parts, order):
    total = parts[0].astype(jnp.float32)
    for s in order:
        total = total + parts[s].astype(jnp.float32)
    return total


def body(initial_rates, stimulus, tile_values, tile_rows, tile_cols, tile_count, cotangent):
    slot_count, tile_width = tile_values.shape[:2]
    batch, owned_width = initial_rates.shape
    own_tiles = owned_width // tile_width
    row_parts, col_parts = lax.axis_size("row"), lax.axis_size("col")
    dense = dense_weights(
        tile_values,
        tile_rows,
        tile_cols,
        tile_count,
        own_tiles,
        row_parts * owned_width,
        col_parts * owned_width,
    )
    turned = transposed(dense)
    col_order, row_order = start_order("col"), start_order("row")
    col_cuts, row_cuts = [(s,) for s in range(col_parts)], [(s,) for s in range(row_parts)]
    rates = initial_rates
    sent_list = []
    active_list = []
    for step_index in range(STEPS - 1):
        sent = gather_relative(rates.astype(jnp.bfloat16) if step_index else rates, "col")
        sent_list.append([(x, 0) for x in sent])
        order = [sent[s] for s in [0] + col_order[::-1]]
        weights, axis = (turned, 0) if step_index else (dense, 1)
        rider = None if step_index else (TWIN, cotangent)
        pieces = multiply(sent_list[-1], order, weights, axis, row_cuts, rider)
        parts = reduce_relative(pieces, "row")
        if rider:
            twin_rider = parts[TWIN]
            parts[TWIN] = twin_rider[:batch]
        current = total_of(parts, row_order)
        active_list.append(jnp.tanh(current + stimulus[step_index].astype(jnp.float32)))
        rates = rates + step_ratio * (active_list[-1] - rates)
    sent = gather_relative(rates.astype(jnp.bfloat16), "col")
    sent_list.append([(x, 0) for x in sent])
    order = [sent[s] for s in [0] + col_order[::-1]]
    cuts = [(s, s ^ TWIN) for s in range(row_parts)]
    pieces = multiply(
        sent_list[-1], order, turned, 0, cuts, stimulus=stimulus[STEPS - 1]
    )
    received = reduce_relative(pieces, "row")
    last_active, pair = turn(
        pieces[0], [received[s] for s in row_order], cotangent, twin_rider
    )
    chosen = [None] * row_parts
    for s in range(row_parts):
        if not s & TWIN:
            both = partner(pair, "row", s) if s else pair
            chosen[s], chosen[s ^ TWIN] = (both, 0), (both, 1)
    order = [x for x, column in chosen if column == 0]
    adjoint = cotangent
    delta_list = [None] * STEPS
    for step_index in reversed(range(STEPS)):
        if step_index < STEPS - 1:
            adjoint = step_ratio * adjoint + total_of(terms, col_order)
            delta = step_ratio * adjoint * (1.0 - active_list[step_index] ** 2)
            gathered = gather_relative(delta.astype(jnp.bfloat16), "row")
            chosen = [(x, 0) for x in gathered]
            order = [gathered[s] for s in [0] + row_order[::-1]]
        delta_list[step_index] = chosen
        terms = reduce_relative(multiply(chosen, order, dense, 0, col_cuts), "col")
    gradient, rates = last_outputs(
        delta_list,
        sent_list,
        tile_rows,
        tile_cols,
        tile_count,
        rates,
        last_active,
        slot_count,
        own_tiles,
    )
    adjoint = step_ratio * adjoint + total_of(terms, col_order)
    return (rates, adjoint, gradient)


def solution(mesh):
    return jax.shard_map(
        body,
        mesh=mesh,
        in_specs=(
            P("group", ("col", "row")),
            P(None, "group", ("col", "row")),
            P(("col", "row"), None, None),
            P(("col", "row"), None),
            P(("col", "row"), None),
            P(("col", "row")),
            P("group", ("col", "row")),
        ),
        out_specs=(
            P("group", ("col", "row")),
            P("group", ("col", "row")),
            P(("group", "col", "row"), None, None),
        ),
        check_vma=False,
    )
```

```python
import math

import jax
import jax.numpy as jnp
from jax import lax
from jax.experimental import pallas as pl
from jax.experimental.pallas import tpu as pltpu
from jax.sharding import PartitionSpec as P

STEPS = 3
TWIN = 2
MIB = 1 << 20

step_ratio = 0.5


def partner(value, axis, shift):
    size = lax.axis_size(axis)
    return lax.ppermute(value, axis, [(index, index ^ shift) for index in range(size)])


def gather_relative(value, axis):
    size = lax.axis_size(axis)
    received = {s: partner(value, axis, s) for s in reversed(range(1, size))}
    return [value] + [received[s] for s in range(1, size)]


def reduce_relative(pieces, axis):
    size = lax.axis_size(axis)
    received = {s: partner(pieces[s], axis, s) for s in range(1, size)}
    return [pieces[0]] + [received[s] for s in range(1, size)]


def in_vmem(count):
    return [pl.BlockSpec(memory_space=pltpu.VMEM)] * count


def in_smem(count):
    return [pl.BlockSpec(memory_space=pltpu.SMEM)] * count


def relative(tile, place, own_tiles):
    return lax.bitwise_xor(tile, place * own_tiles)


def tile_slice(index, tile_width):
    return pl.ds(pl.multiple_of(index * tile_width, tile_width), tile_width)


def in_hbm(value):
    return pltpu.with_memory_space_constraint(value, pltpu.HBM)


def index_copies(rows_hbm, cols_hbm, rows_ref, cols_ref, sems):
    return [
        pltpu.make_async_copy(rows_hbm, rows_ref, sems.at[0]),
        pltpu.make_async_copy(cols_hbm, cols_ref, sems.at[1]),
    ]


def dense_weights(tile_values, rows, cols, count, own_tiles, row_width, col_width):
    slot_count, tile_width = tile_values.shape[:2]
    across = col_width // tile_width
    positions = row_width // tile_width * across
    chunk = slot_count // math.gcd(slot_count, 8)

    def kernel(count_ref, rows_hbm, cols_hbm, values_hbm, dense_ref, slots_ref, *scratch):
        values, rows_ref, cols_ref, value_sems, index_sems = scratch
        indices = index_copies(rows_hbm, cols_hbm, rows_ref, cols_ref, index_sems)
        loads = [
            pltpu.make_async_copy(
                values_hbm.at[first : first + chunk],
                values.at[first : first + chunk],
                value_sems.at[first // chunk],
            )
            for first in range(0, slot_count, chunk)
        ]
        for copy in indices + loads:
            copy.start()
        dense_ref[...] = jnp.zeros_like(dense_ref)

        def clear(position, carry):
            slots_ref[0, position] = -1
            return carry

        lax.fori_loop(0, positions, clear, 0)
        for copy in indices:
            copy.wait()
        row_place, col_place = lax.axis_index("row"), lax.axis_index("col")

        def store(slot, carry):
            row = relative(rows_ref[0, slot], row_place, own_tiles)
            col = relative(cols_ref[0, slot], col_place, own_tiles)
            slots_ref[0, row * across + col] = slot
            dense_ref[tile_slice(row, tile_width), tile_slice(col, tile_width)] = values[slot]
            return carry

        for number, copy in enumerate(loads):
            copy.wait()
            first = number * chunk
            last = jnp.clip(count_ref[0], first, first + chunk)
            lax.fori_loop(first, last, store, 0)

    return pl.pallas_call(
        kernel,
        out_shape=[
            jax.ShapeDtypeStruct((row_width, col_width), jnp.bfloat16),
            pltpu.SMEM((1, positions), jnp.int32),
        ],
        in_specs=in_smem(1) + [pl.BlockSpec(memory_space=pltpu.HBM)] * 3,
        out_specs=in_vmem(1) + in_smem(1),
        scratch_shapes=[
            pltpu.VMEM(tile_values.shape, tile_values.dtype),
            pltpu.SMEM(rows.shape, rows.dtype),
            pltpu.SMEM(cols.shape, cols.dtype),
            pltpu.SemaphoreType.DMA((slot_count // chunk,)),
            pltpu.SemaphoreType.DMA((2,)),
        ],
        compiler_params=pltpu.CompilerParams(
            vmem_limit_bytes=2 * (row_width * col_width + tile_values.size) + 4 * MIB
        ),
    )(count, in_hbm(rows), in_hbm(cols), in_hbm(tile_values))


def start_order(axis):
    size = lax.axis_size(axis)
    far = [2, 3, 1] if axis == "row" else [3, 2, 1]
    return [s for s in range(size - 1, 3, -1)] + [s for s in far if s < size]


def transposed(dense):
    def kernel(dense_ref, out_ref):
        out_ref[...] = dense_ref[...].T

    return pl.pallas_call(
        kernel,
        out_shape=jax.ShapeDtypeStruct(dense.shape[::-1], dense.dtype),
        in_specs=in_vmem(1),
        out_specs=pl.BlockSpec(memory_space=pltpu.VMEM),
        compiler_params=pltpu.CompilerParams(vmem_limit_bytes=8 * dense.size + 8 * MIB),
        cost_estimate=pl.CostEstimate(
            flops=0, bytes_accessed=4 * dense.size, transcendentals=0
        ),
    )(dense)


def multiply(blocks, order, dense, cuts, rider=None, stimulus=None):
    batch, width = order[0].shape[0], dense.shape[0] // len(blocks)
    out_width = dense.shape[1]
    extras = [x for x in (rider[1] if rider else None, stimulus) if x is not None]

    def kernel(*refs):
        dense_ref = refs[len(order)]
        outs = refs[len(order) + 1 + len(extras) :]
        parts = []
        for array, column in blocks:
            ref = refs[[x is array for x in order].index(True)]
            parts.append(ref[:, column * width : (column + 1) * width].astype(jnp.bfloat16))
        whole = jnp.concatenate(parts, axis=1)
        pieces = {}
        for index in range(out_width // width):
            span = slice(index * width, (index + 1) * width)
            pieces[index] = jnp.dot(whole, dense_ref[:, span], preferred_element_type=jnp.float32)
        if stimulus is not None:
            pieces[0] = pieces[0] + refs[len(order) + len(extras)][...].astype(jnp.float32)
        for number, (cut, out) in enumerate(zip(cuts, outs)):
            for place, index in enumerate(cut):
                span = slice(place * width, (place + 1) * width)
                out[:batch, span] = pieces[index].astype(out.dtype)
            if rider and rider[0] == number:
                out[batch:, :] = refs[len(order) + 1][...].astype(out.dtype)

    out_shape = []
    for number, cut in enumerate(cuts):
        rows = 2 * batch if rider and rider[0] == number else batch
        kind = jnp.bfloat16 if number else jnp.float32
        out_shape.append(jax.ShapeDtypeStruct((rows, len(cut) * width), kind))
    return pl.pallas_call(
        kernel,
        out_shape=out_shape,
        in_specs=in_vmem(len(order) + 1 + len(extras)),
        out_specs=in_vmem(len(out_shape)),
        compiler_params=pltpu.CompilerParams(vmem_limit_bytes=2 * dense.size + 8 * MIB),
        cost_estimate=pl.CostEstimate(
            flops=2 * batch * dense.size, bytes_accessed=2 * dense.size, transcendentals=0
        ),
    )(*order, dense, *extras)


def turn(kept, received, cotangent, rider):
    batch, width = cotangent.shape

    def kernel(*refs):
        kept_ref, cotangent_ref, rider_ref, active_ref, delta_ref = refs[len(received) :]
        current = kept_ref[...]
        for ref in refs[: len(received)]:
            current = current + ref[...].astype(jnp.float32)
        active = jnp.tanh(current)
        slope = step_ratio * (1.0 - active**2)
        active_ref[...] = active[:, :width]
        delta_ref[:, :width] = (cotangent_ref[...] * slope[:, :width]).astype(jnp.bfloat16)
        there = rider_ref[batch:, :].astype(jnp.float32)
        delta_ref[:, width:] = (there * slope[:, width:]).astype(jnp.bfloat16)

    return pl.pallas_call(
        kernel,
        out_shape=[
            jax.ShapeDtypeStruct((batch, width), jnp.float32),
            jax.ShapeDtypeStruct((batch, 2 * width), jnp.bfloat16),
        ],
        in_specs=in_vmem(len(received) + 3),
        out_specs=in_vmem(2),
        compiler_params=pltpu.CompilerParams(vmem_limit_bytes=8 * MIB),
        cost_estimate=pl.CostEstimate(
            flops=16 * batch * width,
            bytes_accessed=16 * batch * width,
            transcendentals=2 * batch * width,
        ),
    )(*received, kept, cotangent, rider)


def last_outputs(delta_blocks, sent_blocks, slots, count, rates, active, slot_count, own_tiles):
    steps, (batch, width) = len(delta_blocks), rates.shape
    tile_width = width // own_tiles
    row_parts, col_parts = len(delta_blocks[0]), len(sent_blocks[0])
    operands = []
    for step in delta_blocks + sent_blocks:
        for array, _ in step:
            if not any(array is x for x in operands):
                operands.append(array)
    row_width, col_width = row_parts * width, col_parts * width

    def stack(side, blocks, inputs):
        for step, parts in enumerate(blocks):
            for part, (array, column) in enumerate(parts):
                ref = inputs[[x is array for x in operands].index(True)]
                side[
                    step * batch : (step + 1) * batch, part * width : (part + 1) * width
                ] = ref[:, column * width : (column + 1) * width].astype(jnp.bfloat16)

    def kernel(count_ref, slots_ref, *refs):
        inputs = refs[: len(operands)]
        rates_ref, active_ref, out_ref, last_rates_ref = refs[len(operands) : len(operands) + 4]
        left, right, empty, last_rates, out_sem, rate_sem, *dense = refs[len(operands) + 4 :]
        empty[...] = jnp.zeros_like(empty)

        def dead(slot, carry):
            pltpu.make_async_copy(empty, out_ref.at[slot], out_sem).start()
            return carry

        lax.fori_loop(count_ref[0], slot_count, dead, 0)
        last_rates[...] = rates_ref[...] + step_ratio * (active_ref[...] - rates_ref[...])
        rate_copy = pltpu.make_async_copy(last_rates, last_rates_ref, rate_sem)
        rate_copy.start()
        stack(left, delta_blocks, inputs)
        stack(right, sent_blocks, inputs)
        across = col_parts * own_tiles
        for part, block in enumerate(dense):
            block[...] = lax.dot_general(
                left[:, part * width : (part + 1) * width],
                right[...],
                (((0,), (0,)), ((), ())),
                preferred_element_type=jnp.float32,
            ).astype(jnp.bfloat16)

            def live(col, carry):
                for row in range(own_tiles):
                    slot = slots_ref[0, (part * own_tiles + row) * across + col]
                    tile = block.at[
                        row * tile_width : (row + 1) * tile_width, tile_slice(col, tile_width)
                    ]

                    @pl.when(slot >= 0)
                    def _():
                        pltpu.make_async_copy(tile, out_ref.at[slot], out_sem).start()

                return carry

            lax.fori_loop(0, across, live, 0, unroll=8)
        rate_copy.wait()
        pltpu.make_async_copy(out_ref, out_ref, out_sem).wait()

    total = 2 * row_width * col_width + 8 * steps * batch * (row_width + col_width)
    total += 4 * width * col_width
    return pl.pallas_call(
        kernel,
        out_shape=[
            jax.ShapeDtypeStruct((slot_count, tile_width, tile_width), jnp.bfloat16),
            jax.ShapeDtypeStruct(rates.shape, jnp.float32),
        ],
        in_specs=in_smem(2) + in_vmem(len(operands) + 2),
        out_specs=[pl.BlockSpec(memory_space=pltpu.HBM)] * 2,
        scratch_shapes=[
            pltpu.VMEM((steps * batch, row_width), jnp.bfloat16),
            pltpu.VMEM((steps * batch, col_width), jnp.bfloat16),
            pltpu.VMEM((tile_width, tile_width), jnp.bfloat16),
            pltpu.VMEM(rates.shape, jnp.float32),
            pltpu.SemaphoreType.DMA,
            pltpu.SemaphoreType.DMA,
        ]
        + [pltpu.VMEM((width, col_width), jnp.bfloat16)] * row_parts,
        compiler_params=pltpu.CompilerParams(vmem_limit_bytes=total + 8 * MIB),
    )(count, slots, *operands, rates, active)


def total_of(parts, order):
    total = parts[0].astype(jnp.float32)
    for s in order:
        total = total + parts[s].astype(jnp.float32)
    return total


def body(initial_rates, stimulus, tile_values, tile_rows, tile_cols, tile_count, cotangent):
    slot_count, tile_width = tile_values.shape[:2]
    batch, owned_width = initial_rates.shape
    own_tiles = owned_width // tile_width
    row_parts, col_parts = lax.axis_size("row"), lax.axis_size("col")
    dense, slots = dense_weights(
        tile_values,
        tile_rows,
        tile_cols,
        tile_count,
        own_tiles,
        row_parts * owned_width,
        col_parts * owned_width,
    )
    turned = transposed(dense)
    col_order, row_order = start_order("col"), start_order("row")
    col_cuts, row_cuts = [(s,) for s in range(col_parts)], [(s,) for s in range(row_parts)]
    rates = initial_rates
    sent_list = []
    active_list = []
    for step_index in range(STEPS - 1):
        sent = gather_relative(rates.astype(jnp.bfloat16) if step_index else rates, "col")
        sent_list.append([(x, 0) for x in sent])
        order = [sent[s] for s in [0] + col_order[::-1]]
        rider = None if step_index else (TWIN, cotangent)
        pieces = multiply(sent_list[-1], order, turned, row_cuts, rider)
        parts = reduce_relative(pieces, "row")
        if rider:
            twin_rider = parts[TWIN]
            parts[TWIN] = twin_rider[:batch]
        current = total_of(parts, row_order)
        active_list.append(jnp.tanh(current + stimulus[step_index].astype(jnp.float32)))
        rates = rates + step_ratio * (active_list[-1] - rates)
    sent = gather_relative(rates.astype(jnp.bfloat16), "col")
    sent_list.append([(x, 0) for x in sent])
    order = [sent[s] for s in [0] + col_order[::-1]]
    cuts = [(s, s ^ TWIN) for s in range(row_parts)]
    pieces = multiply(sent_list[-1], order, turned, cuts, stimulus=stimulus[STEPS - 1])
    received = reduce_relative(pieces, "row")
    last_active, pair = turn(
        pieces[0], [received[s] for s in row_order], cotangent, twin_rider
    )
    chosen = [None] * row_parts
    for s in range(row_parts):
        if not s & TWIN:
            both = partner(pair, "row", s) if s else pair
            chosen[s], chosen[s ^ TWIN] = (both, 0), (both, 1)
    order = [x for x, column in chosen if column == 0]
    adjoint = cotangent
    delta_list = [None] * STEPS
    for step_index in reversed(range(STEPS)):
        if step_index < STEPS - 1:
            adjoint = step_ratio * adjoint + total_of(terms, col_order)
            delta = step_ratio * adjoint * (1.0 - active_list[step_index] ** 2)
            gathered = gather_relative(delta.astype(jnp.bfloat16), "row")
            chosen = [(x, 0) for x in gathered]
            order = [gathered[s] for s in [0] + row_order[::-1]]
        delta_list[step_index] = chosen
        terms = reduce_relative(multiply(chosen, order, dense, col_cuts), "col")
    gradient, rates = last_outputs(
        delta_list,
        sent_list,
        slots,
        tile_count,
        rates,
        last_active,
        slot_count,
        own_tiles,
    )
    adjoint = step_ratio * adjoint + total_of(terms, col_order)
    return (rates, adjoint, gradient)


def solution(mesh):
    return jax.shard_map(
        body,
        mesh=mesh,
        in_specs=(
            P("group", ("col", "row")),
            P(None, "group", ("col", "row")),
            P(("col", "row"), None, None),
            P(("col", "row"), None),
            P(("col", "row"), None),
            P(("col", "row")),
            P("group", ("col", "row")),
        ),
        out_specs=(
            P("group", ("col", "row")),
            P("group", ("col", "row")),
            P(("group", "col", "row"), None, None),
        ),
        check_vma=False,
    )
```

```python
import math

import jax
import jax.numpy as jnp
from jax import lax
from jax.experimental import pallas as pl
from jax.experimental.pallas import tpu as pltpu
from jax.sharding import PartitionSpec as P

STEPS = 3
TWIN = 2
MIB = 1 << 20

step_ratio = 0.5


def partner(value, axis, shift):
    size = lax.axis_size(axis)
    return lax.ppermute(value, axis, [(index, index ^ shift) for index in range(size)])


def gather_relative(value, axis):
    size = lax.axis_size(axis)
    received = {s: partner(value, axis, s) for s in reversed(range(1, size))}
    return [value] + [received[s] for s in range(1, size)]


def reduce_relative(pieces, axis):
    size = lax.axis_size(axis)
    received = {s: partner(pieces[s], axis, s) for s in range(1, size)}
    return [pieces[0]] + [received[s] for s in range(1, size)]


def in_vmem(count):
    return [pl.BlockSpec(memory_space=pltpu.VMEM)] * count


def in_smem(count):
    return [pl.BlockSpec(memory_space=pltpu.SMEM)] * count


def relative(tile, place, own_tiles):
    return lax.bitwise_xor(tile, place * own_tiles)


def tile_slice(index, tile_width):
    return pl.ds(pl.multiple_of(index * tile_width, tile_width), tile_width)


def in_hbm(value):
    return pltpu.with_memory_space_constraint(value, pltpu.HBM)


def index_copies(rows_hbm, cols_hbm, rows_ref, cols_ref, sems):
    return [
        pltpu.make_async_copy(rows_hbm, rows_ref, sems.at[0]),
        pltpu.make_async_copy(cols_hbm, cols_ref, sems.at[1]),
    ]


def dense_weights(tile_values, rows, cols, count, own_tiles, row_width, col_width):
    slot_count, tile_width = tile_values.shape[:2]
    across = col_width // tile_width
    positions = row_width // tile_width * across
    chunk = slot_count // math.gcd(slot_count, 8)

    def kernel(count_ref, rows_hbm, cols_hbm, values_hbm, dense_ref, slots_ref, *scratch):
        values, rows_ref, cols_ref, value_sems, index_sems = scratch
        indices = index_copies(rows_hbm, cols_hbm, rows_ref, cols_ref, index_sems)
        loads = [
            pltpu.make_async_copy(
                values_hbm.at[first : first + chunk],
                values.at[first : first + chunk],
                value_sems.at[first // chunk],
            )
            for first in range(0, slot_count, chunk)
        ]
        for copy in indices + loads:
            copy.start()
        dense_ref[...] = jnp.zeros_like(dense_ref)

        def clear(position, carry):
            slots_ref[0, position] = -1
            return carry

        lax.fori_loop(0, positions, clear, 0)
        for copy in indices:
            copy.wait()
        row_place, col_place = lax.axis_index("row"), lax.axis_index("col")

        def store(slot, carry):
            row = relative(rows_ref[0, slot], row_place, own_tiles)
            col = relative(cols_ref[0, slot], col_place, own_tiles)
            slots_ref[0, row * across + col] = slot
            dense_ref[tile_slice(row, tile_width), tile_slice(col, tile_width)] = values[slot]
            return carry

        for number, copy in enumerate(loads):
            copy.wait()
            first = number * chunk
            last = jnp.clip(count_ref[0], first, first + chunk)
            lax.fori_loop(first, last, store, 0)

    return pl.pallas_call(
        kernel,
        out_shape=[
            jax.ShapeDtypeStruct((row_width, col_width), jnp.bfloat16),
            pltpu.SMEM((1, positions), jnp.int32),
        ],
        in_specs=in_smem(1) + [pl.BlockSpec(memory_space=pltpu.HBM)] * 3,
        out_specs=in_vmem(1) + in_smem(1),
        scratch_shapes=[
            pltpu.VMEM(tile_values.shape, tile_values.dtype),
            pltpu.SMEM(rows.shape, rows.dtype),
            pltpu.SMEM(cols.shape, cols.dtype),
            pltpu.SemaphoreType.DMA((slot_count // chunk,)),
            pltpu.SemaphoreType.DMA((2,)),
        ],
        compiler_params=pltpu.CompilerParams(
            vmem_limit_bytes=2 * (row_width * col_width + tile_values.size) + 4 * MIB
        ),
    )(count, in_hbm(rows), in_hbm(cols), in_hbm(tile_values))


def start_order(axis):
    size = lax.axis_size(axis)
    far = [2, 3, 1] if axis == "row" else [3, 2, 1]
    return [s for s in range(size - 1, 3, -1)] + [s for s in far if s < size]


def transposed(dense):
    def kernel(dense_ref, out_ref):
        out_ref[...] = dense_ref[...].T

    return pl.pallas_call(
        kernel,
        out_shape=jax.ShapeDtypeStruct(dense.shape[::-1], dense.dtype),
        in_specs=in_vmem(1),
        out_specs=pl.BlockSpec(memory_space=pltpu.VMEM),
        compiler_params=pltpu.CompilerParams(vmem_limit_bytes=8 * dense.size + 8 * MIB),
        cost_estimate=pl.CostEstimate(
            flops=0, bytes_accessed=4 * dense.size, transcendentals=0
        ),
    )(dense)


def arrays_of(blocks, taken):
    found = []
    for s in taken:
        if not any(blocks[s][0] is x for x in found):
            found.append(blocks[s][0])
    return found


def dot_blocks(blocks, taken, arrays, refs, dense_ref, width, span, total):
    for s in taken:
        array, column = blocks[s]
        ref = refs[[x is array for x in arrays].index(True)]
        term = jnp.dot(
            ref[:, column * width : (column + 1) * width].astype(jnp.bfloat16),
            dense_ref[s * width : (s + 1) * width, span],
            preferred_element_type=jnp.float32,
        )
        total = term if total is None else total + term
    return total


def product_params(blocks, taken, batch, dense):
    size = dense.size * len(taken) // len(blocks)
    return {
        "compiler_params": pltpu.CompilerParams(vmem_limit_bytes=2 * dense.size + 8 * MIB),
        "cost_estimate": pl.CostEstimate(
            flops=2 * batch * size, bytes_accessed=2 * size, transcendentals=0
        ),
    }


def multiply_early(blocks, taken, dense):
    batch, width = blocks[0][0].shape[0], dense.shape[0] // len(blocks)
    arrays = arrays_of(blocks, taken)

    def kernel(*refs):
        *ins, dense_ref, out_ref = refs
        out_ref[...] = dot_blocks(
            blocks, taken, arrays, ins, dense_ref, width, slice(None), None
        )

    return pl.pallas_call(
        kernel,
        out_shape=jax.ShapeDtypeStruct((batch, dense.shape[1]), jnp.float32),
        in_specs=in_vmem(len(arrays) + 1),
        out_specs=pl.BlockSpec(memory_space=pltpu.VMEM),
        **product_params(blocks, taken, batch, dense),
    )(*arrays, dense)


CODE_ROWS = 8
CODE_TOP = 32000.0
CODE_STEPS = 256.0


def encode(arrays):
    whole, rest = [], 0.0
    place = lax.broadcasted_iota(jnp.int32, (CODE_ROWS, arrays[0].shape[1]), 0)
    for number, values in enumerate(arrays):
        largest = jnp.max(jnp.abs(values), axis=0, keepdims=True) + 1e-30
        exponent = jnp.floor(jnp.log2(largest))
        unit = jnp.exp2(exponent)
        mantissa = jnp.ceil(largest / unit * (CODE_STEPS * 1.0001))
        whole.append(jnp.floor(values * (CODE_TOP * CODE_STEPS / (mantissa * unit)) + 0.5))
        rest = jnp.where(place == 2 * number, exponent, rest)
        rest = jnp.where(place == 2 * number + 1, mantissa, rest)
    return jnp.concatenate(whole + [rest], axis=0).astype(jnp.int32).astype(jnp.int16)


def decode(coded, batch, number=0):
    rest = coded[coded.shape[0] - CODE_ROWS :].astype(jnp.float32)
    exponent, mantissa = rest[2 * number : 2 * number + 1], rest[2 * number + 1 : 2 * number + 2]
    step = mantissa * jnp.exp2(exponent) * (1.0 / (CODE_TOP * CODE_STEPS))
    return coded[number * batch : (number + 1) * batch].astype(jnp.float32) * step


def multiply(early, blocks, taken, dense, cuts, coded, rider=None, stimulus=None):
    batch, width = blocks[0][0].shape[0], dense.shape[0] // len(blocks)
    out_width = dense.shape[1]
    arrays = arrays_of(blocks, taken)
    extras = [x for x in (rider[1] if rider else None, stimulus) if x is not None]

    def kernel(*refs):
        dense_ref, early_ref = refs[len(arrays) : len(arrays) + 2]
        more = refs[len(arrays) + 2 : len(arrays) + 2 + len(extras)]
        outs = refs[len(arrays) + 2 + len(extras) :]
        pieces = {}
        for index in range(out_width // width):
            span = slice(index * width, (index + 1) * width)
            pieces[index] = dot_blocks(
                blocks, taken, arrays, refs, dense_ref, width, span, early_ref[:, span]
            )
        if stimulus is not None:
            pieces[0] = pieces[0] + more[-1][STEPS - 1].astype(jnp.float32)
        for number, (cut, out) in enumerate(zip(cuts, outs)):
            for place, index in enumerate(cut):
                span = slice(place * width, (place + 1) * width)
                if coded and number:
                    below = [more[0][...]] if rider and rider[0] == number else []
                    out[:, span] = encode([pieces[index]] + below)
                else:
                    out[:, span] = pieces[index].astype(out.dtype)

    out_shape = []
    for number, cut in enumerate(cuts):
        rows = 2 * batch if rider and rider[0] == number else batch
        rows = rows + CODE_ROWS if coded and number else rows
        sent = jnp.int16 if coded else jnp.bfloat16
        shape = (rows, len(cut) * width)
        out_shape.append(jax.ShapeDtypeStruct(shape, sent if number else jnp.float32))
    return pl.pallas_call(
        kernel,
        out_shape=out_shape,
        in_specs=in_vmem(len(arrays) + 2 + len(extras)),
        out_specs=in_vmem(len(out_shape)),
        **product_params(blocks, taken, batch, dense),
    )(*arrays, dense, early, *extras)


def advance(parts, order, stimulus, rates, step):
    batch = rates.shape[0]

    def kernel(*refs):
        kept_ref, stimulus_ref, rates_ref, active_ref, next_ref, sent_ref = refs[len(order) :]
        current = kept_ref[...] + stimulus_ref[step].astype(jnp.float32)
        for ref in refs[: len(order)]:
            current = current + decode(ref[...], batch)
        active = jnp.tanh(current)
        active_ref[...] = active
        after = rates_ref[...] + step_ratio * (active - rates_ref[...])
        next_ref[...] = after
        sent_ref[...] = after.astype(jnp.bfloat16)

    return pl.pallas_call(
        kernel,
        out_shape=[
            jax.ShapeDtypeStruct(rates.shape, jnp.float32),
            jax.ShapeDtypeStruct(rates.shape, jnp.float32),
            jax.ShapeDtypeStruct(rates.shape, jnp.bfloat16),
        ],
        in_specs=in_vmem(len(order) + 3),
        out_specs=in_vmem(3),
        **small_params(rates.size),
    )(*[parts[s] for s in order], parts[0], stimulus, rates)


def turn(parts, order, cotangent, ridden):
    batch, width = cotangent.shape

    def kernel(*refs):
        kept_ref, cotangent_ref, ridden_ref, active_ref, delta_ref = refs[len(order) :]
        current = kept_ref[...]
        for ref in refs[: len(order)]:
            current = current + decode(ref[...], batch)
        active = jnp.tanh(current)
        active_ref[...] = active[:, :width]
        slope = step_ratio * (1.0 - active**2)
        delta_ref[:, :width] = (cotangent_ref[...] * slope[:, :width]).astype(jnp.bfloat16)
        there = decode(ridden_ref[...], batch, 1)
        delta_ref[:, width:] = (there * slope[:, width:]).astype(jnp.bfloat16)

    return pl.pallas_call(
        kernel,
        out_shape=[
            jax.ShapeDtypeStruct(cotangent.shape, jnp.float32),
            jax.ShapeDtypeStruct(parts[0].shape, jnp.bfloat16),
        ],
        in_specs=in_vmem(len(order) + 3),
        out_specs=in_vmem(2),
        **small_params(parts[0].size),
    )(*[parts[s] for s in order], parts[0], cotangent, ridden)


def small_params(size):
    return {
        "compiler_params": pltpu.CompilerParams(vmem_limit_bytes=8 * MIB),
        "cost_estimate": pl.CostEstimate(
            flops=20 * size, bytes_accessed=16 * size, transcendentals=size
        ),
    }


def last_outputs(delta_blocks, sent_blocks, slots, count, rates, active, slot_count, own_tiles):
    steps, (batch, width) = len(delta_blocks), rates.shape
    tile_width = width // own_tiles
    row_parts, col_parts = len(delta_blocks[0]), len(sent_blocks[0])
    operands = []
    for step in delta_blocks + sent_blocks:
        for array, _ in step:
            if not any(array is x for x in operands):
                operands.append(array)
    row_width, col_width = row_parts * width, col_parts * width

    def stack(side, blocks, inputs):
        for step, parts in enumerate(blocks):
            for part, (array, column) in enumerate(parts):
                ref = inputs[[x is array for x in operands].index(True)]
                side[
                    step * batch : (step + 1) * batch, part * width : (part + 1) * width
                ] = ref[:, column * width : (column + 1) * width].astype(jnp.bfloat16)

    def kernel(count_ref, slots_ref, *refs):
        inputs = refs[: len(operands)]
        rates_ref, active_ref, out_ref, last_rates_ref = refs[len(operands) : len(operands) + 4]
        left, right, empty, last_rates, out_sem, rate_sem, *dense = refs[len(operands) + 4 :]
        empty[...] = jnp.zeros_like(empty)

        def dead(slot, carry):
            pltpu.make_async_copy(empty, out_ref.at[slot], out_sem).start()
            return carry

        lax.fori_loop(count_ref[0], slot_count, dead, 0)
        last_rates[...] = rates_ref[...] + step_ratio * (active_ref[...] - rates_ref[...])
        rate_copy = pltpu.make_async_copy(last_rates, last_rates_ref, rate_sem)
        rate_copy.start()
        stack(left, delta_blocks, inputs)
        stack(right, sent_blocks, inputs)
        across = col_parts * own_tiles
        for part, block in enumerate(dense):
            block[...] = lax.dot_general(
                left[:, part * width : (part + 1) * width],
                right[...],
                (((0,), (0,)), ((), ())),
                preferred_element_type=jnp.float32,
            ).astype(jnp.bfloat16)

            def live(col, carry):
                for row in range(own_tiles):
                    slot = slots_ref[0, (part * own_tiles + row) * across + col]
                    tile = block.at[
                        row * tile_width : (row + 1) * tile_width, tile_slice(col, tile_width)
                    ]

                    @pl.when(slot >= 0)
                    def _():
                        pltpu.make_async_copy(tile, out_ref.at[slot], out_sem).start()

                return carry

            lax.fori_loop(0, across, live, 0, unroll=8)
        rate_copy.wait()
        pltpu.make_async_copy(out_ref, out_ref, out_sem).wait()

    total = 2 * row_width * col_width + 8 * steps * batch * (row_width + col_width)
    total += 4 * width * col_width
    return pl.pallas_call(
        kernel,
        out_shape=[
            jax.ShapeDtypeStruct((slot_count, tile_width, tile_width), jnp.bfloat16),
            jax.ShapeDtypeStruct(rates.shape, jnp.float32),
        ],
        in_specs=in_smem(2) + in_vmem(len(operands) + 2),
        out_specs=[pl.BlockSpec(memory_space=pltpu.HBM)] * 2,
        scratch_shapes=[
            pltpu.VMEM((steps * batch, row_width), jnp.bfloat16),
            pltpu.VMEM((steps * batch, col_width), jnp.bfloat16),
            pltpu.VMEM((tile_width, tile_width), jnp.bfloat16),
            pltpu.VMEM(rates.shape, jnp.float32),
            pltpu.SemaphoreType.DMA,
            pltpu.SemaphoreType.DMA,
        ]
        + [pltpu.VMEM((width, col_width), jnp.bfloat16)] * row_parts,
        compiler_params=pltpu.CompilerParams(vmem_limit_bytes=total + 8 * MIB),
    )(count, slots, *operands, rates, active)


def total_of(parts, order):
    total = parts[0].astype(jnp.float32)
    for s in order:
        total = total + parts[s].astype(jnp.float32)
    return total


def body(initial_rates, stimulus, tile_values, tile_rows, tile_cols, tile_count, cotangent):
    slot_count, tile_width = tile_values.shape[:2]
    batch, owned_width = initial_rates.shape
    own_tiles = owned_width // tile_width
    row_parts, col_parts = lax.axis_size("row"), lax.axis_size("col")
    dense, slots = dense_weights(
        tile_values,
        tile_rows,
        tile_cols,
        tile_count,
        own_tiles,
        row_parts * owned_width,
        col_parts * owned_width,
    )
    turned = transposed(dense)
    col_order, row_order = start_order("col"), start_order("row")
    col_soon, col_late = [0] + col_order[:1], col_order[1:][::-1]
    row_soon, row_late = [0] + row_order[:1], row_order[1:][::-1]
    col_cuts, row_cuts = [(s,) for s in range(col_parts)], [(s,) for s in range(row_parts)]
    rates = initial_rates
    sent_list = []
    active_list = []
    for step_index in range(STEPS - 1):
        sent = gather_relative(rounded if step_index else rates, "col")
        sent_list.append([(x, 0) for x in sent])
        early = multiply_early(sent_list[-1], col_soon, turned)
        rider = None if step_index else (TWIN, cotangent)
        pieces = multiply(early, sent_list[-1], col_late, turned, row_cuts, True, rider)
        parts = reduce_relative(pieces, "row")
        if rider:
            ridden = parts[TWIN]
        active, rates, rounded = advance(parts, row_order, stimulus, rates, step_index)
        active_list.append(active)
    sent = gather_relative(rounded, "col")
    sent_list.append([(x, 0) for x in sent])
    early = multiply_early(sent_list[-1], col_soon, turned)
    cuts = [(s, s ^ TWIN) for s in range(row_parts)]
    pieces = multiply(
        early, sent_list[-1], col_late, turned, cuts, True, None, stimulus
    )
    last_active, pair = turn(reduce_relative(pieces, "row"), row_order, cotangent, ridden)
    chosen = [None] * row_parts
    for s in range(row_parts):
        if s < s ^ TWIN:
            both = partner(pair, "row", s) if s else pair
            chosen[s], chosen[s ^ TWIN] = (both, 0), (both, 1)
    soon = [0, TWIN]
    late = [s for s in range(row_parts) if s not in soon]
    adjoint = cotangent
    delta_list = [None] * STEPS
    for step_index in reversed(range(STEPS)):
        if step_index < STEPS - 1:
            adjoint = step_ratio * adjoint + total_of(terms, col_order)
            delta = step_ratio * adjoint * (1.0 - active_list[step_index] ** 2)
            gathered = gather_relative(delta.astype(jnp.bfloat16), "row")
            chosen = [(x, 0) for x in gathered]
            soon, late = row_soon, row_late
        delta_list[step_index] = chosen
        early = multiply_early(chosen, soon, dense)
        terms = reduce_relative(multiply(early, chosen, late, dense, col_cuts, False), "col")
    gradient, rates = last_outputs(
        delta_list,
        sent_list,
        slots,
        tile_count,
        rates,
        last_active,
        slot_count,
        own_tiles,
    )
    adjoint = step_ratio * adjoint + total_of(terms, col_order)
    return (rates, adjoint, gradient)


def solution(mesh):
    return jax.shard_map(
        body,
        mesh=mesh,
        in_specs=(
            P("group", ("col", "row")),
            P(None, "group", ("col", "row")),
            P(("col", "row"), None, None),
            P(("col", "row"), None),
            P(("col", "row"), None),
            P(("col", "row")),
            P("group", ("col", "row")),
        ),
        out_specs=(
            P("group", ("col", "row")),
            P("group", ("col", "row")),
            P(("group", "col", "row"), None, None),
        ),
        check_vma=False,
    )
```

```python
import math

import jax
import jax.numpy as jnp
from jax import lax
from jax.experimental import pallas as pl
from jax.experimental.pallas import tpu as pltpu
from jax.sharding import PartitionSpec as P

STEPS = 3
TWIN = 2
MIB = 1 << 20

step_ratio = 0.5


def partner(value, axis, shift):
    size = lax.axis_size(axis)
    return lax.ppermute(value, axis, [(index, index ^ shift) for index in range(size)])


def gather_relative(value, axis):
    size = lax.axis_size(axis)
    received = {s: partner(value, axis, s) for s in reversed(range(1, size))}
    return [value] + [received[s] for s in range(1, size)]


def reduce_relative(pieces, axis):
    size = lax.axis_size(axis)
    received = {s: partner(pieces[s], axis, s) for s in range(1, size)}
    return [pieces[0]] + [received[s] for s in range(1, size)]


def in_vmem(count):
    return [pl.BlockSpec(memory_space=pltpu.VMEM)] * count


def in_smem(count):
    return [pl.BlockSpec(memory_space=pltpu.SMEM)] * count


def relative(tile, place, own_tiles):
    return lax.bitwise_xor(tile, place * own_tiles)


def tile_slice(index, tile_width):
    return pl.ds(pl.multiple_of(index * tile_width, tile_width), tile_width)


def in_hbm(value):
    return pltpu.with_memory_space_constraint(value, pltpu.HBM)


def index_copies(rows_hbm, cols_hbm, rows_ref, cols_ref, sems):
    return [
        pltpu.make_async_copy(rows_hbm, rows_ref, sems.at[0]),
        pltpu.make_async_copy(cols_hbm, cols_ref, sems.at[1]),
    ]


def dense_weights(tile_values, rows, cols, count, own_tiles, row_width, col_width):
    slot_count, tile_width = tile_values.shape[:2]
    across = col_width // tile_width
    positions = row_width // tile_width * across
    chunk = slot_count // math.gcd(slot_count, 8)

    def kernel(count_ref, rows_hbm, cols_hbm, values_hbm, dense_ref, slots_ref, *scratch):
        values, rows_ref, cols_ref, value_sems, index_sems = scratch
        indices = index_copies(rows_hbm, cols_hbm, rows_ref, cols_ref, index_sems)
        loads = [
            pltpu.make_async_copy(
                values_hbm.at[first : first + chunk],
                values.at[first : first + chunk],
                value_sems.at[first // chunk],
            )
            for first in range(0, slot_count, chunk)
        ]
        for copy in indices + loads:
            copy.start()
        dense_ref[...] = jnp.zeros_like(dense_ref)

        def clear(position, carry):
            slots_ref[0, position] = -1
            return carry

        lax.fori_loop(0, positions, clear, 0)
        for copy in indices:
            copy.wait()
        row_place, col_place = lax.axis_index("row"), lax.axis_index("col")

        def store(slot, carry):
            row = relative(rows_ref[0, slot], row_place, own_tiles)
            col = relative(cols_ref[0, slot], col_place, own_tiles)
            slots_ref[0, row * across + col] = slot
            dense_ref[tile_slice(row, tile_width), tile_slice(col, tile_width)] = values[slot]
            return carry

        for number, copy in enumerate(loads):
            copy.wait()
            first = number * chunk
            last = jnp.clip(count_ref[0], first, first + chunk)
            lax.fori_loop(first, last, store, 0)

    return pl.pallas_call(
        kernel,
        out_shape=[
            jax.ShapeDtypeStruct((row_width, col_width), jnp.bfloat16),
            pltpu.SMEM((1, positions), jnp.int32),
        ],
        in_specs=in_smem(1) + [pl.BlockSpec(memory_space=pltpu.HBM)] * 3,
        out_specs=in_vmem(1) + in_smem(1),
        scratch_shapes=[
            pltpu.VMEM(tile_values.shape, tile_values.dtype),
            pltpu.SMEM(rows.shape, rows.dtype),
            pltpu.SMEM(cols.shape, cols.dtype),
            pltpu.SemaphoreType.DMA((slot_count // chunk,)),
            pltpu.SemaphoreType.DMA((2,)),
        ],
        compiler_params=pltpu.CompilerParams(
            vmem_limit_bytes=2 * (row_width * col_width + tile_values.size) + 4 * MIB
        ),
    )(count, in_hbm(rows), in_hbm(cols), in_hbm(tile_values))


def start_order(axis, near=(3, 2, 1)):
    size = lax.axis_size(axis)
    return [s for s in range(size - 1, 3, -1)] + [s for s in near if s < size]


def transposed(dense):
    def kernel(dense_ref, out_ref):
        out_ref[...] = dense_ref[...].T

    return pl.pallas_call(
        kernel,
        out_shape=jax.ShapeDtypeStruct(dense.shape[::-1], dense.dtype),
        in_specs=in_vmem(1),
        out_specs=pl.BlockSpec(memory_space=pltpu.VMEM),
        compiler_params=pltpu.CompilerParams(vmem_limit_bytes=8 * dense.size + 8 * MIB),
        cost_estimate=pl.CostEstimate(
            flops=0, bytes_accessed=4 * dense.size, transcendentals=0
        ),
    )(dense)


def arrays_of(blocks, taken):
    found = []
    for s in taken:
        if not any(blocks[s][0] is x for x in found):
            found.append(blocks[s][0])
    return found


def dot_blocks(blocks, taken, arrays, refs, dense_ref, width, span, total):
    for s in taken:
        array, column = blocks[s]
        ref = refs[[x is array for x in arrays].index(True)]
        term = jnp.dot(
            ref[:, column * width : (column + 1) * width].astype(jnp.bfloat16),
            dense_ref[s * width : (s + 1) * width, span],
            preferred_element_type=jnp.float32,
        )
        total = term if total is None else total + term
    return total


def product_params(blocks, taken, batch, dense):
    size = dense.size * len(taken) // len(blocks)
    return {
        "compiler_params": pltpu.CompilerParams(vmem_limit_bytes=2 * dense.size + 8 * MIB),
        "cost_estimate": pl.CostEstimate(
            flops=2 * batch * size, bytes_accessed=2 * size, transcendentals=0
        ),
    }


def multiply_early(blocks, taken, dense):
    batch, width = blocks[0][0].shape[0], dense.shape[0] // len(blocks)
    arrays = arrays_of(blocks, taken)

    def kernel(*refs):
        *ins, dense_ref, out_ref = refs
        out_ref[...] = dot_blocks(
            blocks, taken, arrays, ins, dense_ref, width, slice(None), None
        )

    return pl.pallas_call(
        kernel,
        out_shape=jax.ShapeDtypeStruct((batch, dense.shape[1]), jnp.float32),
        in_specs=in_vmem(len(arrays) + 1),
        out_specs=pl.BlockSpec(memory_space=pltpu.VMEM),
        **product_params(blocks, taken, batch, dense),
    )(*arrays, dense)


CODE_ROWS = 8
CODE_TOP = 32000.0
CODE_STEPS = 256.0


def encode(arrays):
    whole, rest = [], 0.0
    place = lax.broadcasted_iota(jnp.int32, (CODE_ROWS, arrays[0].shape[1]), 0)
    for number, values in enumerate(arrays):
        largest = jnp.max(jnp.abs(values), axis=0, keepdims=True) + 1e-30
        exponent = jnp.floor(jnp.log2(largest))
        unit = jnp.exp2(exponent)
        mantissa = jnp.ceil(largest / unit * (CODE_STEPS * 1.0001))
        whole.append(jnp.floor(values * (CODE_TOP * CODE_STEPS / (mantissa * unit)) + 0.5))
        rest = jnp.where(place == 2 * number, exponent, rest)
        rest = jnp.where(place == 2 * number + 1, mantissa, rest)
    return jnp.concatenate(whole + [rest], axis=0).astype(jnp.int32).astype(jnp.int16)


def decode(coded, batch, number=0):
    rest = coded[coded.shape[0] - CODE_ROWS :].astype(jnp.float32)
    exponent, mantissa = rest[2 * number : 2 * number + 1], rest[2 * number + 1 : 2 * number + 2]
    step = mantissa * jnp.exp2(exponent) * (1.0 / (CODE_TOP * CODE_STEPS))
    return coded[number * batch : (number + 1) * batch].astype(jnp.float32) * step


def multiply(early, blocks, taken, dense, cuts, coded, rider=None, stimulus=None):
    batch, width = blocks[0][0].shape[0], dense.shape[0] // len(blocks)
    out_width = dense.shape[1]
    arrays = arrays_of(blocks, taken)
    extras = [x for x in (rider[1] if rider else None, stimulus) if x is not None]

    def kernel(*refs):
        dense_ref, early_ref = refs[len(arrays) : len(arrays) + 2]
        more = refs[len(arrays) + 2 : len(arrays) + 2 + len(extras)]
        outs = refs[len(arrays) + 2 + len(extras) :]
        pieces = {}
        for index in range(out_width // width):
            span = slice(index * width, (index + 1) * width)
            pieces[index] = dot_blocks(
                blocks, taken, arrays, refs, dense_ref, width, span, early_ref[:, span]
            )
        if stimulus is not None:
            pieces[0] = pieces[0] + more[-1][STEPS - 1].astype(jnp.float32)
        for number, (cut, out) in enumerate(zip(cuts, outs)):
            for place, index in enumerate(cut):
                span = slice(place * width, (place + 1) * width)
                if coded and number:
                    below = [more[0][...]] if rider and rider[0] == number else []
                    out[:, span] = encode([pieces[index]] + below)
                else:
                    out[:, span] = pieces[index].astype(out.dtype)

    out_shape = []
    for number, cut in enumerate(cuts):
        rows = 2 * batch if rider and rider[0] == number else batch
        rows = rows + CODE_ROWS if coded and number else rows
        sent = jnp.int16 if coded else jnp.bfloat16
        shape = (rows, len(cut) * width)
        out_shape.append(jax.ShapeDtypeStruct(shape, sent if number else jnp.float32))
    return pl.pallas_call(
        kernel,
        out_shape=out_shape,
        in_specs=in_vmem(len(arrays) + 2 + len(extras)),
        out_specs=in_vmem(len(out_shape)),
        **product_params(blocks, taken, batch, dense),
    )(*arrays, dense, early, *extras)


def advance(parts, order, stimulus, rates, step):
    batch = rates.shape[0]

    def kernel(*refs):
        kept_ref, stimulus_ref, rates_ref, active_ref, next_ref, sent_ref = refs[len(order) :]
        current = kept_ref[...] + stimulus_ref[step].astype(jnp.float32)
        for ref in refs[: len(order)]:
            current = current + decode(ref[...], batch)
        active = jnp.tanh(current)
        active_ref[...] = active
        after = rates_ref[...] + step_ratio * (active - rates_ref[...])
        next_ref[...] = after
        sent_ref[...] = after.astype(jnp.bfloat16)

    return pl.pallas_call(
        kernel,
        out_shape=[
            jax.ShapeDtypeStruct(rates.shape, jnp.float32),
            jax.ShapeDtypeStruct(rates.shape, jnp.float32),
            jax.ShapeDtypeStruct(rates.shape, jnp.bfloat16),
        ],
        in_specs=in_vmem(len(order) + 3),
        out_specs=in_vmem(3),
        **small_params(rates.size),
    )(*[parts[s] for s in order], parts[0], stimulus, rates)


def turn(parts, order, cotangent, ridden):
    batch, width = cotangent.shape

    def kernel(*refs):
        kept_ref, cotangent_ref, ridden_ref, active_ref, delta_ref = refs[len(order) :]
        current = kept_ref[...]
        for ref in refs[: len(order)]:
            current = current + decode(ref[...], batch)
        active = jnp.tanh(current)
        active_ref[...] = active[:, :width]
        slope = step_ratio * (1.0 - active**2)
        delta_ref[:, :width] = (cotangent_ref[...] * slope[:, :width]).astype(jnp.bfloat16)
        there = decode(ridden_ref[...], batch, 1)
        delta_ref[:, width:] = (there * slope[:, width:]).astype(jnp.bfloat16)

    return pl.pallas_call(
        kernel,
        out_shape=[
            jax.ShapeDtypeStruct(cotangent.shape, jnp.float32),
            jax.ShapeDtypeStruct(parts[0].shape, jnp.bfloat16),
        ],
        in_specs=in_vmem(len(order) + 3),
        out_specs=in_vmem(2),
        **small_params(parts[0].size),
    )(*[parts[s] for s in order], parts[0], cotangent, ridden)


def small_params(size):
    return {
        "compiler_params": pltpu.CompilerParams(vmem_limit_bytes=8 * MIB),
        "cost_estimate": pl.CostEstimate(
            flops=20 * size, bytes_accessed=16 * size, transcendentals=size
        ),
    }


def last_outputs(delta_blocks, sent_blocks, slots, count, rates, active, slot_count, own_tiles):
    steps, (batch, width) = len(delta_blocks), rates.shape
    tile_width = width // own_tiles
    row_parts, col_parts = len(delta_blocks[0]), len(sent_blocks[0])
    operands = []
    for step in delta_blocks + sent_blocks:
        for array, _ in step:
            if not any(array is x for x in operands):
                operands.append(array)
    row_width, col_width = row_parts * width, col_parts * width

    def stack(side, blocks, inputs):
        for step, parts in enumerate(blocks):
            for part, (array, column) in enumerate(parts):
                ref = inputs[[x is array for x in operands].index(True)]
                side[
                    step * batch : (step + 1) * batch, part * width : (part + 1) * width
                ] = ref[:, column * width : (column + 1) * width].astype(jnp.bfloat16)

    def kernel(count_ref, slots_ref, *refs):
        inputs = refs[: len(operands)]
        rates_ref, active_ref, out_ref, last_rates_ref = refs[len(operands) : len(operands) + 4]
        left, right, empty, last_rates, out_sem, rate_sem, *dense = refs[len(operands) + 4 :]
        empty[...] = jnp.zeros_like(empty)

        def dead(slot, carry):
            pltpu.make_async_copy(empty, out_ref.at[slot], out_sem).start()
            return carry

        lax.fori_loop(count_ref[0], slot_count, dead, 0)
        last_rates[...] = rates_ref[...] + step_ratio * (active_ref[...] - rates_ref[...])
        rate_copy = pltpu.make_async_copy(last_rates, last_rates_ref, rate_sem)
        rate_copy.start()
        stack(left, delta_blocks, inputs)
        stack(right, sent_blocks, inputs)
        across = col_parts * own_tiles
        for part, block in enumerate(dense):
            block[...] = lax.dot_general(
                left[:, part * width : (part + 1) * width],
                right[...],
                (((0,), (0,)), ((), ())),
                preferred_element_type=jnp.float32,
            ).astype(jnp.bfloat16)

            def live(col, carry):
                for row in range(own_tiles):
                    slot = slots_ref[0, (part * own_tiles + row) * across + col]
                    tile = block.at[
                        row * tile_width : (row + 1) * tile_width, tile_slice(col, tile_width)
                    ]

                    @pl.when(slot >= 0)
                    def _():
                        pltpu.make_async_copy(tile, out_ref.at[slot], out_sem).start()

                return carry

            lax.fori_loop(0, across, live, 0, unroll=8)
        rate_copy.wait()
        pltpu.make_async_copy(out_ref, out_ref, out_sem).wait()

    total = 2 * row_width * col_width + 8 * steps * batch * (row_width + col_width)
    total += 4 * width * col_width
    return pl.pallas_call(
        kernel,
        out_shape=[
            jax.ShapeDtypeStruct((slot_count, tile_width, tile_width), jnp.bfloat16),
            jax.ShapeDtypeStruct(rates.shape, jnp.float32),
        ],
        in_specs=in_smem(2) + in_vmem(len(operands) + 2),
        out_specs=[pl.BlockSpec(memory_space=pltpu.HBM)] * 2,
        scratch_shapes=[
            pltpu.VMEM((steps * batch, row_width), jnp.bfloat16),
            pltpu.VMEM((steps * batch, col_width), jnp.bfloat16),
            pltpu.VMEM((tile_width, tile_width), jnp.bfloat16),
            pltpu.VMEM(rates.shape, jnp.float32),
            pltpu.SemaphoreType.DMA,
            pltpu.SemaphoreType.DMA,
        ]
        + [pltpu.VMEM((width, col_width), jnp.bfloat16)] * row_parts,
        compiler_params=pltpu.CompilerParams(vmem_limit_bytes=total + 8 * MIB),
    )(count, slots, *operands, rates, active)


def total_of(parts, order):
    total = parts[0].astype(jnp.float32)
    for s in order:
        total = total + parts[s].astype(jnp.float32)
    return total


def body(initial_rates, stimulus, tile_values, tile_rows, tile_cols, tile_count, cotangent):
    slot_count, tile_width = tile_values.shape[:2]
    batch, owned_width = initial_rates.shape
    own_tiles = owned_width // tile_width
    row_parts, col_parts = lax.axis_size("row"), lax.axis_size("col")
    dense, slots = dense_weights(
        tile_values,
        tile_rows,
        tile_cols,
        tile_count,
        own_tiles,
        row_parts * owned_width,
        col_parts * owned_width,
    )
    turned = transposed(dense)
    col_order, row_order, back_order = (
        start_order("col"),
        start_order("row", (2, 3, 1)),
        start_order("row"),
    )
    col_soon, col_late = [0] + col_order[:1], col_order[1:][::-1]
    row_soon, row_late = [0] + back_order[:1], back_order[1:][::-1]
    col_cuts, row_cuts = [(s,) for s in range(col_parts)], [(s,) for s in range(row_parts)]
    rates = initial_rates
    sent_list = []
    active_list = []
    for step_index in range(STEPS - 1):
        sent = gather_relative(rounded if step_index else rates, "col")
        sent_list.append([(x, 0) for x in sent])
        early = multiply_early(sent_list[-1], col_soon, turned)
        rider = (TWIN, cotangent) if step_index else None
        pieces = multiply(early, sent_list[-1], col_late, turned, row_cuts, True, rider)
        parts = reduce_relative(pieces, "row")
        if rider:
            ridden = parts[TWIN]
        active, rates, rounded = advance(parts, row_order, stimulus, rates, step_index)
        active_list.append(active)
    sent = gather_relative(rounded, "col")
    sent_list.append([(x, 0) for x in sent])
    early = multiply_early(sent_list[-1], col_soon, turned)
    cuts = [(s, s ^ TWIN) for s in range(row_parts)]
    pieces = multiply(
        early, sent_list[-1], col_late, turned, cuts, True, None, stimulus
    )
    last_active, pair = turn(reduce_relative(pieces, "row"), back_order, cotangent, ridden)
    chosen = [None] * row_parts
    for s in range(row_parts):
        if s < s ^ TWIN:
            both = partner(pair, "row", s) if s else pair
            chosen[s], chosen[s ^ TWIN] = (both, 0), (both, 1)
    soon = [0, TWIN]
    late = [s for s in range(row_parts) if s not in soon]
    adjoint = cotangent
    delta_list = [None] * STEPS
    for step_index in reversed(range(STEPS)):
        if step_index < STEPS - 1:
            adjoint = step_ratio * adjoint + total_of(terms, col_order)
            delta = step_ratio * adjoint * (1.0 - active_list[step_index] ** 2)
            gathered = gather_relative(delta.astype(jnp.bfloat16), "row")
            chosen = [(x, 0) for x in gathered]
            soon, late = row_soon, row_late
        delta_list[step_index] = chosen
        early = multiply_early(chosen, soon, dense)
        terms = reduce_relative(multiply(early, chosen, late, dense, col_cuts, False), "col")
    gradient, rates = last_outputs(
        delta_list,
        sent_list,
        slots,
        tile_count,
        rates,
        last_active,
        slot_count,
        own_tiles,
    )
    adjoint = step_ratio * adjoint + total_of(terms, col_order)
    return (rates, adjoint, gradient)


def solution(mesh):
    return jax.shard_map(
        body,
        mesh=mesh,
        in_specs=(
            P("group", ("col", "row")),
            P(None, "group", ("col", "row")),
            P(("col", "row"), None, None),
            P(("col", "row"), None),
            P(("col", "row"), None),
            P(("col", "row")),
            P("group", ("col", "row")),
        ),
        out_specs=(
            P("group", ("col", "row")),
            P("group", ("col", "row")),
            P(("group", "col", "row"), None, None),
        ),
        check_vma=False,
    )
```

```python
import math

import jax
import jax.numpy as jnp
from jax import lax
from jax.experimental import pallas as pl
from jax.experimental.pallas import tpu as pltpu
from jax.sharding import PartitionSpec as P

STEPS = 3
TWIN = 2
MIB = 1 << 20

step_ratio = 0.5


def partner(value, axis, shift):
    size = lax.axis_size(axis)
    return lax.ppermute(value, axis, [(index, index ^ shift) for index in range(size)])


def gather_relative(value, axis):
    size = lax.axis_size(axis)
    received = {s: partner(value, axis, s) for s in reversed(range(1, size))}
    return [value] + [received[s] for s in range(1, size)]


def reduce_relative(pieces, axis):
    size = lax.axis_size(axis)
    received = {s: partner(pieces[s], axis, s) for s in range(1, size)}
    return [pieces[0]] + [received[s] for s in range(1, size)]


def in_vmem(count):
    return [pl.BlockSpec(memory_space=pltpu.VMEM)] * count


def in_smem(count):
    return [pl.BlockSpec(memory_space=pltpu.SMEM)] * count


def relative(tile, place, own_tiles):
    return lax.bitwise_xor(tile, place * own_tiles)


def tile_slice(index, tile_width):
    return pl.ds(pl.multiple_of(index * tile_width, tile_width), tile_width)


def in_hbm(value):
    return pltpu.with_memory_space_constraint(value, pltpu.HBM)


def index_copies(rows_hbm, cols_hbm, rows_ref, cols_ref, sems):
    return [
        pltpu.make_async_copy(rows_hbm, rows_ref, sems.at[0]),
        pltpu.make_async_copy(cols_hbm, cols_ref, sems.at[1]),
    ]


def dense_weights(tile_values, rows, cols, count, own_tiles, row_width, col_width):
    slot_count, tile_width = tile_values.shape[:2]
    across = col_width // tile_width
    positions = row_width // tile_width * across
    chunk = slot_count // math.gcd(slot_count, 8)

    def kernel(count_ref, rows_hbm, cols_hbm, values_hbm, dense_ref, slots_ref, *scratch):
        values, rows_ref, cols_ref, value_sems, index_sems = scratch
        indices = index_copies(rows_hbm, cols_hbm, rows_ref, cols_ref, index_sems)
        loads = [
            pltpu.make_async_copy(
                values_hbm.at[first : first + chunk],
                values.at[first : first + chunk],
                value_sems.at[first // chunk],
            )
            for first in range(0, slot_count, chunk)
        ]
        for copy in indices + loads:
            copy.start()
        dense_ref[...] = jnp.zeros_like(dense_ref)

        def clear(position, carry):
            slots_ref[0, position] = -1
            return carry

        lax.fori_loop(0, positions, clear, 0)
        for copy in indices:
            copy.wait()
        row_place, col_place = lax.axis_index("row"), lax.axis_index("col")

        def store(slot, carry):
            row = relative(rows_ref[0, slot], row_place, own_tiles)
            col = relative(cols_ref[0, slot], col_place, own_tiles)
            slots_ref[0, row * across + col] = slot
            dense_ref[tile_slice(row, tile_width), tile_slice(col, tile_width)] = values[slot]
            return carry

        for number, copy in enumerate(loads):
            copy.wait()
            first = number * chunk
            last = jnp.clip(count_ref[0], first, first + chunk)
            lax.fori_loop(first, last, store, 0)

    return pl.pallas_call(
        kernel,
        out_shape=[
            jax.ShapeDtypeStruct((row_width, col_width), jnp.bfloat16),
            pltpu.SMEM((1, positions), jnp.int32),
        ],
        in_specs=in_smem(1) + [pl.BlockSpec(memory_space=pltpu.HBM)] * 3,
        out_specs=in_vmem(1) + in_smem(1),
        scratch_shapes=[
            pltpu.VMEM(tile_values.shape, tile_values.dtype),
            pltpu.SMEM(rows.shape, rows.dtype),
            pltpu.SMEM(cols.shape, cols.dtype),
            pltpu.SemaphoreType.DMA((slot_count // chunk,)),
            pltpu.SemaphoreType.DMA((2,)),
        ],
        compiler_params=pltpu.CompilerParams(
            vmem_limit_bytes=2 * (row_width * col_width + tile_values.size) + 4 * MIB
        ),
    )(count, in_hbm(rows), in_hbm(cols), in_hbm(tile_values))


def start_order(axis, near=(3, 2, 1)):
    size = lax.axis_size(axis)
    return [s for s in range(size - 1, 3, -1)] + [s for s in near if s < size]


def transposed(dense):
    def kernel(dense_ref, out_ref):
        out_ref[...] = dense_ref[...].T

    return pl.pallas_call(
        kernel,
        out_shape=jax.ShapeDtypeStruct(dense.shape[::-1], dense.dtype),
        in_specs=in_vmem(1),
        out_specs=pl.BlockSpec(memory_space=pltpu.VMEM),
        compiler_params=pltpu.CompilerParams(vmem_limit_bytes=8 * dense.size + 8 * MIB),
        cost_estimate=pl.CostEstimate(
            flops=0, bytes_accessed=4 * dense.size, transcendentals=0
        ),
    )(dense)


def arrays_of(blocks, taken):
    found = []
    for s in taken:
        if not any(blocks[s][0] is x for x in found):
            found.append(blocks[s][0])
    return found


def dot_blocks(blocks, taken, arrays, refs, dense_ref, width, span, total):
    for s in taken:
        array, column = blocks[s]
        ref = refs[[x is array for x in arrays].index(True)]
        term = jnp.dot(
            ref[:, column * width : (column + 1) * width].astype(jnp.bfloat16),
            dense_ref[s * width : (s + 1) * width, span],
            preferred_element_type=jnp.float32,
        )
        total = term if total is None else total + term
    return total


def product_params(blocks, taken, batch, dense):
    size = dense.size * len(taken) // len(blocks)
    return {
        "compiler_params": pltpu.CompilerParams(vmem_limit_bytes=2 * dense.size + 8 * MIB),
        "cost_estimate": pl.CostEstimate(
            flops=2 * batch * size, bytes_accessed=2 * size, transcendentals=0
        ),
    }


def multiply_early(blocks, taken, dense):
    batch, width = blocks[0][0].shape[0], dense.shape[0] // len(blocks)
    arrays = arrays_of(blocks, taken)

    def kernel(*refs):
        *ins, dense_ref, out_ref = refs
        out_ref[...] = dot_blocks(
            blocks, taken, arrays, ins, dense_ref, width, slice(None), None
        )

    return pl.pallas_call(
        kernel,
        out_shape=jax.ShapeDtypeStruct((batch, dense.shape[1]), jnp.float32),
        in_specs=in_vmem(len(arrays) + 1),
        out_specs=pl.BlockSpec(memory_space=pltpu.VMEM),
        **product_params(blocks, taken, batch, dense),
    )(*arrays, dense)


CODE_ROWS = 8
CODE_TOP = 32000.0
CODE_STEPS = 256.0


def encode(arrays):
    whole, rest = [], 0.0
    place = lax.broadcasted_iota(jnp.int32, (CODE_ROWS, arrays[0].shape[1]), 0)
    for number, values in enumerate(arrays):
        largest = jnp.max(jnp.abs(values), axis=0, keepdims=True) + 1e-30
        exponent = jnp.floor(jnp.log2(largest))
        unit = jnp.exp2(exponent)
        mantissa = jnp.ceil(largest / unit * (CODE_STEPS * 1.0001))
        whole.append(jnp.floor(values * (CODE_TOP * CODE_STEPS / (mantissa * unit)) + 0.5))
        rest = jnp.where(place == 2 * number, exponent, rest)
        rest = jnp.where(place == 2 * number + 1, mantissa, rest)
    return jnp.concatenate(whole + [rest], axis=0).astype(jnp.int32).astype(jnp.int16)


def decode(coded, batch, number=0):
    rest = coded[coded.shape[0] - CODE_ROWS :].astype(jnp.float32)
    exponent, mantissa = rest[2 * number : 2 * number + 1], rest[2 * number + 1 : 2 * number + 2]
    step = mantissa * jnp.exp2(exponent) * (1.0 / (CODE_TOP * CODE_STEPS))
    return coded[number * batch : (number + 1) * batch].astype(jnp.float32) * step


def multiply(early, blocks, taken, dense, cuts, coded, rider=None, stimulus=None):
    batch, width = blocks[0][0].shape[0], dense.shape[0] // len(blocks)
    out_width = dense.shape[1]
    arrays = arrays_of(blocks, taken)
    extras = [x for x in (rider[1] if rider else None, stimulus) if x is not None]

    def kernel(*refs):
        dense_ref, early_ref = refs[len(arrays) : len(arrays) + 2]
        more = refs[len(arrays) + 2 : len(arrays) + 2 + len(extras)]
        outs = refs[len(arrays) + 2 + len(extras) :]
        pieces = {}
        for index in range(out_width // width):
            span = slice(index * width, (index + 1) * width)
            pieces[index] = dot_blocks(
                blocks, taken, arrays, refs, dense_ref, width, span, early_ref[:, span]
            )
        if stimulus is not None:
            pieces[0] = pieces[0] + more[-1][STEPS - 1].astype(jnp.float32)
        for number, (cut, out) in enumerate(zip(cuts, outs)):
            if coded and number:
                below = [more[0][...]] if rider and rider[0] == number else []
                out[...] = encode([pieces[index] for index in cut] + below)
                continue
            for place, index in enumerate(cut):
                span = slice(place * width, (place + 1) * width)
                out[:, span] = pieces[index].astype(out.dtype)

    out_shape = []
    for number, cut in enumerate(cuts):
        shape = (batch, len(cut) * width)
        if coded and number:
            arrays_sent = len(cut) + (1 if rider and rider[0] == number else 0)
            shape = (arrays_sent * batch + CODE_ROWS, width)
        sent = jnp.int16 if coded else jnp.bfloat16
        out_shape.append(jax.ShapeDtypeStruct(shape, sent if number else jnp.float32))
    return pl.pallas_call(
        kernel,
        out_shape=out_shape,
        in_specs=in_vmem(len(arrays) + 2 + len(extras)),
        out_specs=in_vmem(len(out_shape)),
        **product_params(blocks, taken, batch, dense),
    )(*arrays, dense, early, *extras)


def advance(parts, order, stimulus, rates, step):
    batch = rates.shape[0]

    def kernel(*refs):
        kept_ref, stimulus_ref, rates_ref, active_ref, next_ref, sent_ref = refs[len(order) :]
        current = kept_ref[...] + stimulus_ref[step].astype(jnp.float32)
        for ref in refs[: len(order)]:
            current = current + decode(ref[...], batch)
        active = jnp.tanh(current)
        active_ref[...] = active
        after = rates_ref[...] + step_ratio * (active - rates_ref[...])
        next_ref[...] = after
        sent_ref[...] = after.astype(jnp.bfloat16)

    return pl.pallas_call(
        kernel,
        out_shape=[
            jax.ShapeDtypeStruct(rates.shape, jnp.float32),
            jax.ShapeDtypeStruct(rates.shape, jnp.float32),
            jax.ShapeDtypeStruct(rates.shape, jnp.bfloat16),
        ],
        in_specs=in_vmem(len(order) + 3),
        out_specs=in_vmem(3),
        **small_params(rates.size),
    )(*[parts[s] for s in order], parts[0], stimulus, rates)


def turn(parts, order, cotangent, ridden):
    batch, width = cotangent.shape

    def kernel(*refs):
        kept_ref, cotangent_ref, ridden_ref, active_ref, delta_ref = refs[len(order) :]
        for number in range(2):
            span = slice(number * width, (number + 1) * width)
            current = kept_ref[:, span]
            for ref in refs[: len(order)]:
                current = current + decode(ref[...], batch, number)
            active = jnp.tanh(current)
            if number == 0:
                active_ref[...] = active
                left = cotangent_ref[...]
            else:
                left = decode(ridden_ref[...], batch, 1)
            delta_ref[:, span] = (left * (step_ratio * (1.0 - active**2))).astype(jnp.bfloat16)

    return pl.pallas_call(
        kernel,
        out_shape=[
            jax.ShapeDtypeStruct(cotangent.shape, jnp.float32),
            jax.ShapeDtypeStruct(parts[0].shape, jnp.bfloat16),
        ],
        in_specs=in_vmem(len(order) + 3),
        out_specs=in_vmem(2),
        **small_params(parts[0].size),
    )(*[parts[s] for s in order], parts[0], cotangent, ridden)


def small_params(size):
    return {
        "compiler_params": pltpu.CompilerParams(vmem_limit_bytes=8 * MIB),
        "cost_estimate": pl.CostEstimate(
            flops=20 * size, bytes_accessed=16 * size, transcendentals=size
        ),
    }


def last_outputs(delta_blocks, sent_blocks, slots, count, rates, active, slot_count, own_tiles):
    steps, (batch, width) = len(delta_blocks), rates.shape
    tile_width = width // own_tiles
    row_parts, col_parts = len(delta_blocks[0]), len(sent_blocks[0])
    operands = []
    for step in delta_blocks + sent_blocks:
        for array, _ in step:
            if not any(array is x for x in operands):
                operands.append(array)
    row_width, col_width = row_parts * width, col_parts * width

    def stack(side, blocks, inputs):
        for step, parts in enumerate(blocks):
            for part, (array, column) in enumerate(parts):
                ref = inputs[[x is array for x in operands].index(True)]
                side[
                    step * batch : (step + 1) * batch, part * width : (part + 1) * width
                ] = ref[:, column * width : (column + 1) * width].astype(jnp.bfloat16)

    def kernel(count_ref, slots_ref, *refs):
        inputs = refs[: len(operands)]
        rates_ref, active_ref, out_ref, last_rates_ref = refs[len(operands) : len(operands) + 4]
        left, right, empty, last_rates, out_sem, rate_sem, *dense = refs[len(operands) + 4 :]
        empty[...] = jnp.zeros_like(empty)

        def dead(slot, carry):
            pltpu.make_async_copy(empty, out_ref.at[slot], out_sem).start()
            return carry

        lax.fori_loop(count_ref[0], slot_count, dead, 0)
        last_rates[...] = rates_ref[...] + step_ratio * (active_ref[...] - rates_ref[...])
        rate_copy = pltpu.make_async_copy(last_rates, last_rates_ref, rate_sem)
        rate_copy.start()
        stack(left, delta_blocks, inputs)
        stack(right, sent_blocks, inputs)
        across = col_parts * own_tiles
        for part, block in enumerate(dense):
            block[...] = lax.dot_general(
                left[:, part * width : (part + 1) * width],
                right[...],
                (((0,), (0,)), ((), ())),
                preferred_element_type=jnp.float32,
            ).astype(jnp.bfloat16)

            def live(col, carry):
                for row in range(own_tiles):
                    slot = slots_ref[0, (part * own_tiles + row) * across + col]
                    tile = block.at[
                        row * tile_width : (row + 1) * tile_width, tile_slice(col, tile_width)
                    ]

                    @pl.when(slot >= 0)
                    def _():
                        pltpu.make_async_copy(tile, out_ref.at[slot], out_sem).start()

                return carry

            lax.fori_loop(0, across, live, 0, unroll=8)
        rate_copy.wait()
        pltpu.make_async_copy(out_ref, out_ref, out_sem).wait()

    total = 2 * row_width * col_width + 8 * steps * batch * (row_width + col_width)
    total += 4 * width * col_width
    return pl.pallas_call(
        kernel,
        out_shape=[
            jax.ShapeDtypeStruct((slot_count, tile_width, tile_width), jnp.bfloat16),
            jax.ShapeDtypeStruct(rates.shape, jnp.float32),
        ],
        in_specs=in_smem(2) + in_vmem(len(operands) + 2),
        out_specs=[pl.BlockSpec(memory_space=pltpu.HBM)] * 2,
        scratch_shapes=[
            pltpu.VMEM((steps * batch, row_width), jnp.bfloat16),
            pltpu.VMEM((steps * batch, col_width), jnp.bfloat16),
            pltpu.VMEM((tile_width, tile_width), jnp.bfloat16),
            pltpu.VMEM(rates.shape, jnp.float32),
            pltpu.SemaphoreType.DMA,
            pltpu.SemaphoreType.DMA,
        ]
        + [pltpu.VMEM((width, col_width), jnp.bfloat16)] * row_parts,
        compiler_params=pltpu.CompilerParams(vmem_limit_bytes=total + 8 * MIB),
    )(count, slots, *operands, rates, active)


def total_of(parts, order):
    total = parts[0].astype(jnp.float32)
    for s in order:
        total = total + parts[s].astype(jnp.float32)
    return total


def body(initial_rates, stimulus, tile_values, tile_rows, tile_cols, tile_count, cotangent):
    slot_count, tile_width = tile_values.shape[:2]
    batch, owned_width = initial_rates.shape
    own_tiles = owned_width // tile_width
    row_parts, col_parts = lax.axis_size("row"), lax.axis_size("col")
    dense, slots = dense_weights(
        tile_values,
        tile_rows,
        tile_cols,
        tile_count,
        own_tiles,
        row_parts * owned_width,
        col_parts * owned_width,
    )
    turned = transposed(dense)
    col_order, row_order, back_order = (
        start_order("col"),
        start_order("row", (2, 3, 1)),
        start_order("row"),
    )
    col_soon, col_late = [0] + col_order[:1], col_order[1:][::-1]
    row_soon, row_late = [0] + back_order[:1], back_order[1:][::-1]
    col_cuts, row_cuts = [(s,) for s in range(col_parts)], [(s,) for s in range(row_parts)]
    rates = initial_rates
    sent_list = []
    active_list = []
    for step_index in range(STEPS - 1):
        sent = gather_relative(rounded if step_index else rates, "col")
        sent_list.append([(x, 0) for x in sent])
        early = multiply_early(sent_list[-1], col_soon, turned)
        rider = (TWIN, cotangent) if step_index else None
        pieces = multiply(early, sent_list[-1], col_late, turned, row_cuts, True, rider)
        parts = reduce_relative(pieces, "row")
        if rider:
            ridden = parts[TWIN]
        active, rates, rounded = advance(parts, row_order, stimulus, rates, step_index)
        active_list.append(active)
    sent = gather_relative(rounded, "col")
    sent_list.append([(x, 0) for x in sent])
    early = multiply_early(sent_list[-1], col_soon, turned)
    cuts = [(s, s ^ TWIN) for s in range(row_parts)]
    pieces = multiply(
        early, sent_list[-1], col_late, turned, cuts, True, None, stimulus
    )
    last_active, pair = turn(reduce_relative(pieces, "row"), back_order, cotangent, ridden)
    chosen = [None] * row_parts
    for s in range(row_parts):
        if s < s ^ TWIN:
            both = partner(pair, "row", s) if s else pair
            chosen[s], chosen[s ^ TWIN] = (both, 0), (both, 1)
    soon = [0, TWIN]
    late = [s for s in range(row_parts) if s not in soon]
    adjoint = cotangent
    delta_list = [None] * STEPS
    for step_index in reversed(range(STEPS)):
        if step_index < STEPS - 1:
            adjoint = step_ratio * adjoint + total_of(terms, col_order)
            delta = step_ratio * adjoint * (1.0 - active_list[step_index] ** 2)
            gathered = gather_relative(delta.astype(jnp.bfloat16), "row")
            chosen = [(x, 0) for x in gathered]
            soon, late = row_soon, row_late
        delta_list[step_index] = chosen
        early = multiply_early(chosen, soon, dense)
        terms = reduce_relative(multiply(early, chosen, late, dense, col_cuts, False), "col")
    gradient, rates = last_outputs(
        delta_list,
        sent_list,
        slots,
        tile_count,
        rates,
        last_active,
        slot_count,
        own_tiles,
    )
    adjoint = step_ratio * adjoint + total_of(terms, col_order)
    return (rates, adjoint, gradient)


def solution(mesh):
    return jax.shard_map(
        body,
        mesh=mesh,
        in_specs=(
            P("group", ("col", "row")),
            P(None, "group", ("col", "row")),
            P(("col", "row"), None, None),
            P(("col", "row"), None),
            P(("col", "row"), None),
            P(("col", "row")),
            P("group", ("col", "row")),
        ),
        out_specs=(
            P("group", ("col", "row")),
            P("group", ("col", "row")),
            P(("group", "col", "row"), None, None),
        ),
        check_vma=False,
    )
```

```python
import math

import jax
import jax.numpy as jnp
from jax import lax
from jax.experimental import pallas as pl
from jax.experimental.pallas import tpu as pltpu
from jax.sharding import PartitionSpec as P

STEPS = 3
TWIN = 2
MIB = 1 << 20

step_ratio = 0.5


def partner(value, axis, shift):
    size = lax.axis_size(axis)
    return lax.ppermute(value, axis, [(index, index ^ shift) for index in range(size)])


def gather_relative(value, axis):
    size = lax.axis_size(axis)
    received = {s: partner(value, axis, s) for s in reversed(range(1, size))}
    return [value] + [received[s] for s in range(1, size)]


def reduce_relative(pieces, axis):
    size = lax.axis_size(axis)
    received = {s: partner(pieces[s], axis, s) for s in range(1, size)}
    return [pieces[0]] + [received[s] for s in range(1, size)]


def in_vmem(count):
    return [pl.BlockSpec(memory_space=pltpu.VMEM)] * count


def in_smem(count):
    return [pl.BlockSpec(memory_space=pltpu.SMEM)] * count


def relative(tile, place, own_tiles):
    return lax.bitwise_xor(tile, place * own_tiles)


def tile_slice(index, tile_width):
    return pl.ds(pl.multiple_of(index * tile_width, tile_width), tile_width)


def in_hbm(value):
    return pltpu.with_memory_space_constraint(value, pltpu.HBM)


def index_copies(rows_hbm, cols_hbm, rows_ref, cols_ref, sems):
    return [
        pltpu.make_async_copy(rows_hbm, rows_ref, sems.at[0]),
        pltpu.make_async_copy(cols_hbm, cols_ref, sems.at[1]),
    ]


def dense_weights(tile_values, rows, cols, count, own_tiles, row_width, col_width):
    slot_count, tile_width = tile_values.shape[:2]
    across = col_width // tile_width
    positions = row_width // tile_width * across
    chunk = slot_count // math.gcd(slot_count, 8)

    def kernel(count_ref, rows_hbm, cols_hbm, values_hbm, dense_ref, slots_ref, *scratch):
        values, rows_ref, cols_ref, value_sems, index_sems = scratch
        indices = index_copies(rows_hbm, cols_hbm, rows_ref, cols_ref, index_sems)
        loads = [
            pltpu.make_async_copy(
                values_hbm.at[first : first + chunk],
                values.at[first : first + chunk],
                value_sems.at[first // chunk],
            )
            for first in range(0, slot_count, chunk)
        ]
        for copy in indices + loads:
            copy.start()
        dense_ref[...] = jnp.zeros_like(dense_ref)

        def clear(position, carry):
            slots_ref[0, position] = -1
            return carry

        lax.fori_loop(0, positions, clear, 0, unroll=8)
        for copy in indices:
            copy.wait()
        row_place, col_place = lax.axis_index("row"), lax.axis_index("col")

        def store(slot, carry):
            row = relative(rows_ref[0, slot], row_place, own_tiles)
            col = relative(cols_ref[0, slot], col_place, own_tiles)
            slots_ref[0, row * across + col] = slot
            dense_ref[tile_slice(row, tile_width), tile_slice(col, tile_width)] = values[slot]
            return carry

        for number, copy in enumerate(loads):
            copy.wait()
            first = number * chunk
            last = jnp.clip(count_ref[0], first, first + chunk)
            lax.fori_loop(first, last, store, 0)

    return pl.pallas_call(
        kernel,
        out_shape=[
            jax.ShapeDtypeStruct((row_width, col_width), jnp.bfloat16),
            pltpu.SMEM((1, positions), jnp.int32),
        ],
        in_specs=in_smem(1) + [pl.BlockSpec(memory_space=pltpu.HBM)] * 3,
        out_specs=in_vmem(1) + in_smem(1),
        scratch_shapes=[
            pltpu.VMEM(tile_values.shape, tile_values.dtype),
            pltpu.SMEM(rows.shape, rows.dtype),
            pltpu.SMEM(cols.shape, cols.dtype),
            pltpu.SemaphoreType.DMA((slot_count // chunk,)),
            pltpu.SemaphoreType.DMA((2,)),
        ],
        compiler_params=pltpu.CompilerParams(
            vmem_limit_bytes=2 * (row_width * col_width + tile_values.size) + 4 * MIB
        ),
    )(count, in_hbm(rows), in_hbm(cols), in_hbm(tile_values))


def start_order(axis, near=(3, 2, 1)):
    size = lax.axis_size(axis)
    return [s for s in range(size - 1, 3, -1)] + [s for s in near if s < size]


def transposed(dense):
    def kernel(dense_ref, out_ref):
        out_ref[...] = dense_ref[...].T

    return pl.pallas_call(
        kernel,
        out_shape=jax.ShapeDtypeStruct(dense.shape[::-1], dense.dtype),
        in_specs=in_vmem(1),
        out_specs=pl.BlockSpec(memory_space=pltpu.VMEM),
        compiler_params=pltpu.CompilerParams(vmem_limit_bytes=8 * dense.size + 8 * MIB),
        cost_estimate=pl.CostEstimate(
            flops=0, bytes_accessed=4 * dense.size, transcendentals=0
        ),
    )(dense)


def arrays_of(blocks, taken):
    found = []
    for s in taken:
        if not any(blocks[s][0] is x for x in found):
            found.append(blocks[s][0])
    return found


def dot_blocks(blocks, taken, arrays, refs, dense_ref, width, span, total):
    for s in taken:
        array, column = blocks[s]
        ref = refs[[x is array for x in arrays].index(True)]
        term = jnp.dot(
            ref[:, column * width : (column + 1) * width].astype(jnp.bfloat16),
            dense_ref[s * width : (s + 1) * width, span],
            preferred_element_type=jnp.float32,
        )
        total = term if total is None else total + term
    return total


def product_params(blocks, taken, batch, dense):
    size = dense.size * len(taken) // len(blocks)
    return {
        "compiler_params": pltpu.CompilerParams(vmem_limit_bytes=2 * dense.size + 8 * MIB),
        "cost_estimate": pl.CostEstimate(
            flops=2 * batch * size, bytes_accessed=2 * size, transcendentals=0
        ),
    }


def multiply_early(blocks, taken, dense):
    batch, width = blocks[0][0].shape[0], dense.shape[0] // len(blocks)
    arrays = arrays_of(blocks, taken)

    def kernel(*refs):
        *ins, dense_ref, out_ref = refs
        out_ref[...] = dot_blocks(
            blocks, taken, arrays, ins, dense_ref, width, slice(None), None
        )

    return pl.pallas_call(
        kernel,
        out_shape=jax.ShapeDtypeStruct((batch, dense.shape[1]), jnp.float32),
        in_specs=in_vmem(len(arrays) + 1),
        out_specs=pl.BlockSpec(memory_space=pltpu.VMEM),
        **product_params(blocks, taken, batch, dense),
    )(*arrays, dense)


CODE_ROWS = 8
CODE_TOP = 32000.0
CODE_STEPS = 256.0


def encode(arrays):
    whole, rest = [], 0.0
    place = lax.broadcasted_iota(jnp.int32, (CODE_ROWS, arrays[0].shape[1]), 0)
    for number, values in enumerate(arrays):
        largest = jnp.max(jnp.abs(values), axis=0, keepdims=True) + 1e-30
        exponent = jnp.floor(jnp.log2(largest))
        unit = jnp.exp2(exponent)
        mantissa = jnp.ceil(largest / unit * (CODE_STEPS * 1.0001))
        whole.append(jnp.floor(values * (CODE_TOP * CODE_STEPS / (mantissa * unit)) + 0.5))
        rest = jnp.where(place == 2 * number, exponent, rest)
        rest = jnp.where(place == 2 * number + 1, mantissa, rest)
    return jnp.concatenate(whole + [rest], axis=0).astype(jnp.int32).astype(jnp.int16)


def decode(coded, batch, number=0):
    rest = coded[coded.shape[0] - CODE_ROWS :].astype(jnp.float32)
    exponent, mantissa = rest[2 * number : 2 * number + 1], rest[2 * number + 1 : 2 * number + 2]
    step = mantissa * jnp.exp2(exponent) * (1.0 / (CODE_TOP * CODE_STEPS))
    return coded[number * batch : (number + 1) * batch].astype(jnp.float32) * step


def multiply(early, blocks, taken, dense, cuts, coded, rider=None, stimulus=None):
    batch, width = blocks[0][0].shape[0], dense.shape[0] // len(blocks)
    out_width = dense.shape[1]
    arrays = arrays_of(blocks, taken)
    extras = [x for x in (rider[1] if rider else None, stimulus) if x is not None]

    def kernel(*refs):
        dense_ref, early_ref = refs[len(arrays) : len(arrays) + 2]
        more = refs[len(arrays) + 2 : len(arrays) + 2 + len(extras)]
        outs = refs[len(arrays) + 2 + len(extras) :]
        pieces = {}
        for index in range(out_width // width):
            span = slice(index * width, (index + 1) * width)
            pieces[index] = dot_blocks(
                blocks, taken, arrays, refs, dense_ref, width, span, early_ref[:, span]
            )
        if stimulus is not None:
            pieces[0] = pieces[0] + more[-1][STEPS - 1].astype(jnp.float32)
        for number, (cut, out) in enumerate(zip(cuts, outs)):
            if coded and number:
                below = [more[0][...]] if rider and rider[0] == number else []
                out[...] = encode([pieces[index] for index in cut] + below)
                continue
            for place, index in enumerate(cut):
                span = slice(place * width, (place + 1) * width)
                out[:, span] = pieces[index].astype(out.dtype)

    out_shape = []
    for number, cut in enumerate(cuts):
        shape = (batch, len(cut) * width)
        if coded and number:
            arrays_sent = len(cut) + (1 if rider and rider[0] == number else 0)
            shape = (arrays_sent * batch + CODE_ROWS, width)
        sent = jnp.int16 if coded else jnp.bfloat16
        out_shape.append(jax.ShapeDtypeStruct(shape, sent if number else jnp.float32))
    return pl.pallas_call(
        kernel,
        out_shape=out_shape,
        in_specs=in_vmem(len(arrays) + 2 + len(extras)),
        out_specs=in_vmem(len(out_shape)),
        **product_params(blocks, taken, batch, dense),
    )(*arrays, dense, early, *extras)


def advance(parts, order, stimulus, rates, step):
    batch = rates.shape[0]

    def kernel(*refs):
        kept_ref, stimulus_ref, rates_ref, active_ref, next_ref, sent_ref = refs[len(order) :]
        current = kept_ref[...] + stimulus_ref[step].astype(jnp.float32)
        for ref in refs[: len(order)]:
            current = current + decode(ref[...], batch)
        active = jnp.tanh(current)
        active_ref[...] = active
        after = rates_ref[...] + step_ratio * (active - rates_ref[...])
        next_ref[...] = after
        sent_ref[...] = after.astype(jnp.bfloat16)

    return pl.pallas_call(
        kernel,
        out_shape=[
            jax.ShapeDtypeStruct(rates.shape, jnp.float32),
            jax.ShapeDtypeStruct(rates.shape, jnp.float32),
            jax.ShapeDtypeStruct(rates.shape, jnp.bfloat16),
        ],
        in_specs=in_vmem(len(order) + 3),
        out_specs=in_vmem(3),
        **small_params(rates.size),
    )(*[parts[s] for s in order], parts[0], stimulus, rates)


def turn(parts, order, cotangent, ridden):
    batch, width = cotangent.shape

    def kernel(*refs):
        kept_ref, cotangent_ref, ridden_ref, active_ref, delta_ref = refs[len(order) :]
        for number in range(2):
            span = slice(number * width, (number + 1) * width)
            current = kept_ref[:, span]
            for ref in refs[: len(order)]:
                current = current + decode(ref[...], batch, number)
            active = jnp.tanh(current)
            if number == 0:
                active_ref[...] = active
                left = cotangent_ref[...]
            else:
                left = decode(ridden_ref[...], batch, 1)
            delta_ref[:, span] = (left * (step_ratio * (1.0 - active**2))).astype(jnp.bfloat16)

    return pl.pallas_call(
        kernel,
        out_shape=[
            jax.ShapeDtypeStruct(cotangent.shape, jnp.float32),
            jax.ShapeDtypeStruct(parts[0].shape, jnp.bfloat16),
        ],
        in_specs=in_vmem(len(order) + 3),
        out_specs=in_vmem(2),
        **small_params(parts[0].size),
    )(*[parts[s] for s in order], parts[0], cotangent, ridden)


def small_params(size):
    return {
        "compiler_params": pltpu.CompilerParams(vmem_limit_bytes=8 * MIB),
        "cost_estimate": pl.CostEstimate(
            flops=20 * size, bytes_accessed=16 * size, transcendentals=size
        ),
    }


def last_outputs(delta_blocks, sent_blocks, slots, count, rates, active, slot_count, own_tiles):
    steps, (batch, width) = len(delta_blocks), rates.shape
    tile_width = width // own_tiles
    row_parts, col_parts = len(delta_blocks[0]), len(sent_blocks[0])
    operands = []
    for step in delta_blocks + sent_blocks:
        for array, _ in step:
            if not any(array is x for x in operands):
                operands.append(array)
    row_width, col_width = row_parts * width, col_parts * width

    def stack(side, blocks, inputs):
        for step, parts in enumerate(blocks):
            for part, (array, column) in enumerate(parts):
                ref = inputs[[x is array for x in operands].index(True)]
                side[
                    step * batch : (step + 1) * batch, part * width : (part + 1) * width
                ] = ref[:, column * width : (column + 1) * width].astype(jnp.bfloat16)

    def kernel(count_ref, slots_ref, *refs):
        inputs = refs[: len(operands)]
        rates_ref, active_ref, out_ref, last_rates_ref = refs[len(operands) : len(operands) + 4]
        left, right, empty, last_rates, out_sem, rate_sem, *dense = refs[len(operands) + 4 :]
        empty[...] = jnp.zeros_like(empty)

        def dead(slot, carry):
            pltpu.make_async_copy(empty, out_ref.at[slot], out_sem).start()
            return carry

        lax.fori_loop(count_ref[0], slot_count, dead, 0)
        last_rates[...] = rates_ref[...] + step_ratio * (active_ref[...] - rates_ref[...])
        rate_copy = pltpu.make_async_copy(last_rates, last_rates_ref, rate_sem)
        rate_copy.start()
        stack(left, delta_blocks, inputs)
        stack(right, sent_blocks, inputs)
        across = col_parts * own_tiles
        for part, block in enumerate(dense):
            block[...] = lax.dot_general(
                left[:, part * width : (part + 1) * width],
                right[...],
                (((0,), (0,)), ((), ())),
                preferred_element_type=jnp.float32,
            ).astype(jnp.bfloat16)

            def live(col, carry):
                for row in range(own_tiles):
                    slot = slots_ref[0, (part * own_tiles + row) * across + col]
                    tile = block.at[
                        row * tile_width : (row + 1) * tile_width, tile_slice(col, tile_width)
                    ]

                    @pl.when(slot >= 0)
                    def _():
                        pltpu.make_async_copy(tile, out_ref.at[slot], out_sem).start()

                return carry

            lax.fori_loop(0, across, live, 0, unroll=8)
        rate_copy.wait()
        pltpu.make_async_copy(out_ref, out_ref, out_sem).wait()

    total = 2 * row_width * col_width + 8 * steps * batch * (row_width + col_width)
    total += 4 * width * col_width
    return pl.pallas_call(
        kernel,
        out_shape=[
            jax.ShapeDtypeStruct((slot_count, tile_width, tile_width), jnp.bfloat16),
            jax.ShapeDtypeStruct(rates.shape, jnp.float32),
        ],
        in_specs=in_smem(2) + in_vmem(len(operands) + 2),
        out_specs=[pl.BlockSpec(memory_space=pltpu.HBM)] * 2,
        scratch_shapes=[
            pltpu.VMEM((steps * batch, row_width), jnp.bfloat16),
            pltpu.VMEM((steps * batch, col_width), jnp.bfloat16),
            pltpu.VMEM((tile_width, tile_width), jnp.bfloat16),
            pltpu.VMEM(rates.shape, jnp.float32),
            pltpu.SemaphoreType.DMA,
            pltpu.SemaphoreType.DMA,
        ]
        + [pltpu.VMEM((width, col_width), jnp.bfloat16)] * row_parts,
        compiler_params=pltpu.CompilerParams(vmem_limit_bytes=total + 8 * MIB),
    )(count, slots, *operands, rates, active)


def total_of(parts, order):
    total = parts[0].astype(jnp.float32)
    for s in order:
        total = total + parts[s].astype(jnp.float32)
    return total


def body(initial_rates, stimulus, tile_values, tile_rows, tile_cols, tile_count, cotangent):
    slot_count, tile_width = tile_values.shape[:2]
    batch, owned_width = initial_rates.shape
    own_tiles = owned_width // tile_width
    row_parts, col_parts = lax.axis_size("row"), lax.axis_size("col")
    dense, slots = dense_weights(
        tile_values,
        tile_rows,
        tile_cols,
        tile_count,
        own_tiles,
        row_parts * owned_width,
        col_parts * owned_width,
    )
    turned = transposed(dense)
    col_order, row_order, back_order = (
        start_order("col"),
        start_order("row", (2, 3, 1)),
        start_order("row"),
    )
    col_soon, col_late = [0] + col_order[:1], col_order[1:][::-1]
    row_soon, row_late = [0] + back_order[:1], back_order[1:][::-1]
    col_cuts, row_cuts = [(s,) for s in range(col_parts)], [(s,) for s in range(row_parts)]
    rates = initial_rates
    sent_list = []
    active_list = []
    for step_index in range(STEPS - 1):
        sent = gather_relative(rounded if step_index else rates, "col")
        sent_list.append([(x, 0) for x in sent])
        early = multiply_early(sent_list[-1], col_soon, turned)
        rider = (TWIN, cotangent) if step_index else None
        pieces = multiply(early, sent_list[-1], col_late, turned, row_cuts, True, rider)
        parts = reduce_relative(pieces, "row")
        if rider:
            ridden = parts[TWIN]
        active, rates, rounded = advance(parts, row_order, stimulus, rates, step_index)
        active_list.append(active)
    sent = gather_relative(rounded, "col")
    sent_list.append([(x, 0) for x in sent])
    early = multiply_early(sent_list[-1], col_soon, turned)
    cuts = [(s, s ^ TWIN) for s in range(row_parts)]
    pieces = multiply(
        early, sent_list[-1], col_late, turned, cuts, True, None, stimulus
    )
    last_active, pair = turn(reduce_relative(pieces, "row"), back_order, cotangent, ridden)
    chosen = [None] * row_parts
    for s in range(row_parts):
        if s < s ^ TWIN:
            both = partner(pair, "row", s) if s else pair
            chosen[s], chosen[s ^ TWIN] = (both, 0), (both, 1)
    soon = [0, TWIN]
    late = [s for s in range(row_parts) if s not in soon]
    adjoint = cotangent
    delta_list = [None] * STEPS
    for step_index in reversed(range(STEPS)):
        if step_index < STEPS - 1:
            adjoint = step_ratio * adjoint + total_of(terms, col_order)
            delta = step_ratio * adjoint * (1.0 - active_list[step_index] ** 2)
            gathered = gather_relative(delta.astype(jnp.bfloat16), "row")
            chosen = [(x, 0) for x in gathered]
            soon, late = row_soon, row_late
        delta_list[step_index] = chosen
        early = multiply_early(chosen, soon, dense)
        terms = reduce_relative(multiply(early, chosen, late, dense, col_cuts, False), "col")
    gradient, rates = last_outputs(
        delta_list,
        sent_list,
        slots,
        tile_count,
        rates,
        last_active,
        slot_count,
        own_tiles,
    )
    adjoint = step_ratio * adjoint + total_of(terms, col_order)
    return (rates, adjoint, gradient)


def solution(mesh):
    return jax.shard_map(
        body,
        mesh=mesh,
        in_specs=(
            P("group", ("col", "row")),
            P(None, "group", ("col", "row")),
            P(("col", "row"), None, None),
            P(("col", "row"), None),
            P(("col", "row"), None),
            P(("col", "row")),
            P("group", ("col", "row")),
        ),
        out_specs=(
            P("group", ("col", "row")),
            P("group", ("col", "row")),
            P(("group", "col", "row"), None, None),
        ),
        check_vma=False,
    )
```
